32 devices in a mesh: row: 4 (over y, x), col: 8 (over z, core).
Axes of the slice: x: 2, y: 2, z: 4, core: 2. Of those that a mesh axis runs over, the one named last changes fastest.
Arguments:
- sign_iterate: bfloat16 [4096, 4096], P('row', 'col'), may hold values from -6 to 6
- sign_square: bfloat16 [4096, 4096], P('row', 'col'), may hold values from -0.1875 to 0.1875
- pattern_x: int32 [32, 32], P('row', 'col'), may hold values 0 or 1
- pattern_y: int32 [32, 32], P('row', 'col'), may hold values 0 or 1
- pattern_product: int32 [32, 32], P('row', 'col'), may hold values 0 or 1
- orbital_energy: bfloat16 [4096], P('row'), may hold values from -3 to 1
- pair_dest: int32 [32, 32, 1], P(('row', 'col')), may hold values from 0 to 31; in each aligned block of 32 rows (0 to 31, 32 to 63, ..., all dimensions but the last counted through in order) at most 2 rows name the same one
- pair_block: int32 [32, 32], P(('row', 'col')), may hold values from 0 to 31
- force_h: bfloat16 [2048, 128, 128], P(('row', 'col')), may hold values from -0.5 to 0.5
- force_s: bfloat16 [2048, 128, 128], P(('row', 'col')), may hold values from -0.5 to 0.5
Outputs:
- sign_next: bfloat16 [4096, 4096], P('row', 'col')
- forces: float32 [2048], P(('row', 'col'))
The draws below stay inside these ranges and needn't reach their ends.
Inputs may be any that keep to these rules, and one draw needn't show every extreme that they name: `pair_dest`: among the 32 entries of one device no owner is named more than 2 times, a bound that some block reaches. `pair_block`: A row-major index into the device's own 8 x 4 grid of blocks.
All inputs are finite; a program needn't handle non-finite values. No bound on the sum of `pattern_x` or of `pattern_y` or of `pattern_product` on one device may be relied on, other than what follows from the above.
Results may differ from the reference program's by a relative error of at most 0.003.
Values may be sent and summed in bfloat16 or wider, within the bound.
A program may use at most 128 MiB of HBM per device.

```python
import math
import jax
import jax.numpy as jnp
import numpy as np
from jax import lax

BS = 128
QB = 4
CAP = 2
NBT = 32
ORDER = 4096
MB_DEV = 8
BLK_DEV = 32
PAIRS_DEV = 32
N_ROW = 4
N_COL = 8


def touch_ends(result, key, least, largest):
    place = [jax.random.randint(jax.random.fold_in(key, axis), (), 0, length) for axis, length in enumerate(result.shape)]
    longest = result.shape.index(max(result.shape))
    neighbour = place[:longest] + [(place[longest] + 1) % result.shape[longest]] + place[longest + 1:]
    return result.at[tuple(place)].set(least).at[tuple(neighbour)].set(largest)


def levels(stream_key, shape, pieces, low, top_value):
    level, own = 1.0, jax.random.fold_in(stream_key, 6)
    for position, parts in pieces:
        draws = jnp.exp(jax.random.uniform(jax.random.fold_in(own, position), (parts,), jnp.float32, low / len(pieces), top_value / len(pieces)))
        level = level * jnp.repeat(draws, shape[position] // parts).reshape([-1 if axis == position else 1 for axis in range(len(shape))])
    return level


def assign_block(rng, own, number, rows, amount, top, bound, skew):
    ranking = jax.random.permutation(rng, amount)
    heavy_load, ordinary = load_shares(amount, rows * top, bound, skew, True), load_shares(amount, rows * top, bound, skew, False)
    places = jnp.arange(amount)

    def named(tallies, offset_by):
        used = int((tallies > 0).sum())
        fixed = max(1, used // 4)
        moved = fixed + (places - fixed + offset_by * (used - fixed)) % max(1, amount - fixed)
        return jnp.zeros((amount,), jnp.int32).at[ranking[jnp.where(places < fixed, places, moved)]].set(jnp.asarray(tallies, jnp.int32))

    tallies = jnp.where(number % 4 == 0, named(heavy_load, number // 4), named(ordinary, number - number // 4 - 1))
    mixed = jax.random.permutation(jax.random.fold_in(own, 3), amount)
    donor, taker = mixed[0:amount // 2 * 2:2], mixed[1:amount // 2 * 2:2]
    room = jnp.minimum(tallies[donor] - 1, bound - tallies[taker]) // 2
    room = jnp.where((donor == ranking[0]) | (taker == ranking[0]) | (tallies[taker] == 0), 0, jnp.maximum(room, 0))
    moved = jax.random.randint(jax.random.fold_in(own, 4), (amount // 2,), 0, 1 << 20) % (room + 1)
    tallies = tallies.at[donor].add(-moved).at[taker].add(moved)
    members = jnp.searchsorted(jnp.cumsum(tallies), jnp.arange(rows * top), side="right").astype(jnp.int32)
    table = members.reshape(top, rows).T
    table = table[jax.random.permutation(jax.random.fold_in(own, 1), rows)]
    offset_by = jax.random.randint(jax.random.fold_in(own, 2), (rows, 1), 0, top)
    return jnp.take_along_axis(table, (jnp.arange(top)[None, :] + offset_by) % top, axis=1)


def load_shares(number_of, total, limit, lean, full):
    loads = [(1 << 20) // math.isqrt(standing ** lean) + 1 for standing in range(1, number_of + 1)]
    largest = limit if full else min(limit, max(-(-total // number_of), total * loads[0] // sum(loads)))
    least = 1 if total - largest >= number_of - 1 else 0
    holding, surplus = [largest] + [least] * (number_of - 1), total - largest - least * (number_of - 1)
    while surplus > 0:
        movable = [i for i in range(1, number_of) if holding[i] < largest] or [i for i in range(1, number_of) if holding[i] < limit]
        whole, budget = sum([loads[i] for i in movable]), surplus
        for i in movable:
            addition = min(limit - holding[i], max(1, budget * loads[i] // whole), surplus)
            holding[i] = holding[i] + addition
            surplus = surplus - addition
    return np.array(holding)


def bell_draw(rng, dims, width, most, split=(), held_as=jnp.bfloat16):
    level = levels(rng, dims, split, -0.22, 0.18) if split else 1.0
    array = jax.random.normal(rng, dims, jnp.float32) * width * level
    return jnp.minimum(jnp.maximum(array, -most), most).astype(held_as)


def setup_inputs(seed: int = 0) -> dict:
    splits = jax.random.split(jax.random.key(seed), 11)
    sign_iterate = bell_draw(splits[0], (ORDER, ORDER), 1.0, 6.0, ((0, 4), (1, 8)))
    sign_square = bell_draw(splits[1], (ORDER, ORDER), (ORDER // 4) ** -0.5, 0.1875, ((0, 4), (1, 8)))
    pattern_x = touch_ends((jax.random.randint(splits[2], (NBT, NBT), 0, 2) < 1).astype(jnp.int32), jax.random.fold_in(splits[2], 1), 0, 1)
    pattern_y = touch_ends((jax.random.randint(splits[3], (NBT, NBT), 0, 2) < 1).astype(jnp.int32), jax.random.fold_in(splits[3], 1), 0, 1)
    pattern_product = touch_ends((jax.random.randint(splits[4], (NBT, NBT), 0, 4) < 3).astype(jnp.int32), jax.random.fold_in(splits[4], 1), 0, 1)
    orbital_energy = jnp.clip(-3.0 + 4.0 * jax.random.uniform(splits[5], (ORDER,), jnp.float32) ** levels(splits[5], (ORDER,), ((0, 4),), -0.2, 0.2), -3.0, 1.0).astype(jnp.bfloat16)
    pair_dest_keys = jax.random.split(jax.random.fold_in(splits[6], 1), (N_ROW * N_COL) * PAIRS_DEV // PAIRS_DEV)
    pair_dest_turns = jax.random.permutation(jax.random.fold_in(splits[6], 3), (N_ROW * N_COL) * PAIRS_DEV // PAIRS_DEV)
    pair_dest = jax.vmap(lambda own, number: assign_block(jax.random.fold_in(splits[6], 2), own, number, PAIRS_DEV, N_ROW * N_COL, 1, CAP, 2))(pair_dest_keys, pair_dest_turns).reshape((N_ROW * N_COL, PAIRS_DEV, 1))
    pair_block = touch_ends(jax.random.randint(splits[7], (N_ROW * N_COL, PAIRS_DEV), 0, BLK_DEV), jax.random.fold_in(splits[7], 1), 0, BLK_DEV - 1).astype(jnp.int32)
    force_h = bell_draw(splits[8], (N_ROW * N_COL * N_ROW * N_COL * CAP, BS, BS), BS ** -0.5, 0.5, ((0, 32),))
    force_s = bell_draw(splits[9], (N_ROW * N_COL * N_ROW * N_COL * CAP, BS, BS), BS ** -0.5, 0.5, ((0, 32),))
    return {"sign_iterate": sign_iterate, "sign_square": sign_square, "pattern_x": pattern_x, "pattern_y": pattern_y, "pattern_product": pattern_product, "orbital_energy": orbital_energy, "pair_dest": pair_dest, "pair_block": pair_block, "force_h": force_h, "force_s": force_s}


def apply_pattern(matrix, pattern):
    blocks = matrix.reshape(NBT, BS, NBT, BS) * pattern[:, None, :, None].astype(matrix.dtype)
    return blocks.reshape(ORDER, ORDER)


def reference(sign_iterate, sign_square, pattern_x, pattern_y, pattern_product, orbital_energy, pair_dest, pair_block, force_h, force_s):
    xmask = apply_pattern(sign_iterate, pattern_x)
    ymask = apply_pattern(sign_square, pattern_y)
    product = jnp.dot(xmask, ymask, preferred_element_type=jnp.float32)
    product = apply_pattern(product, pattern_product)
    xnew = 1.5 * xmask.astype(jnp.float32) - 0.5 * product
    sign_next = xnew.astype(jnp.bfloat16)
    diag_index = jnp.arange(ORDER)
    half_dens = (-0.5 * xnew).at[diag_index, diag_index].add(0.5)
    density = half_dens.astype(jnp.bfloat16)
    energy_f = orbital_energy.astype(jnp.float32)
    devices = N_ROW * N_COL
    dest = pair_dest[:, :, 0]
    same = dest[:, :, None] == dest[:, None, :]
    earlier = jnp.arange(PAIRS_DEV)[None, :] < jnp.arange(PAIRS_DEV)[:, None]
    rank = jnp.sum((same & earlier[None, :, :]).astype(jnp.int32), axis=2)
    dev_ids = jnp.arange(devices, dtype=jnp.int32)[:, None]
    block_row = (dev_ids // N_COL) * MB_DEV + pair_block // QB
    block_col = (dev_ids % N_COL) * QB + pair_block % QB
    slot = dest * (devices * CAP) + dev_ids * CAP + rank

    def one_pair(item):
        brow, bcol, where = item
        dblk = lax.dynamic_slice(density, (brow * BS, bcol * BS), (BS, BS)).astype(jnp.float32)
        eblk = lax.dynamic_slice_in_dim(energy_f, brow * BS, BS, 0)
        hblk = lax.dynamic_index_in_dim(force_h, where, 0, keepdims=False).astype(jnp.float32)
        sblk = lax.dynamic_index_in_dim(force_s, where, 0, keepdims=False).astype(jnp.float32)
        return jnp.sum(dblk * hblk) - jnp.sum(eblk[:, None] * dblk * sblk)

    values = lax.map(one_pair, (block_row.reshape(-1).astype(jnp.int32), block_col.reshape(-1).astype(jnp.int32), slot.reshape(-1).astype(jnp.int32)))
    forces = jnp.zeros((devices * devices * CAP,), jnp.float32).at[slot.reshape(-1)].set(values)
    return sign_next, forces
```

```python
import jax
import jax.numpy as jnp
from jax import lax
from jax.experimental import pallas as pl
from jax.experimental.pallas import tpu as pltpu
from jax.sharding import PartitionSpec as P

BS = 128
QB = 4
CAP = 2
MESH = pl.DeviceIdType.MESH


def masked_tile(tile, pattern):
    rows, cols = tile.shape
    shaped = tile.reshape(rows // BS, BS, cols // BS, BS) * pattern[:, None, :, None].astype(
        tile.dtype
    )
    return shaped.reshape(rows, cols)


def tile_blocks(tile):
    rows, cols = tile.shape
    shaped = tile.reshape(rows // BS, BS, cols // BS, BS).transpose(0, 2, 1, 3)
    return shaped.reshape(rows // BS * (cols // BS), BS * BS)


def rank_within(dest):
    entries = dest.shape[-1]
    order = jnp.arange(entries, dtype=jnp.int32)
    same = (dest[..., :, None] == dest[..., None, :]) & (order[None, :] < order[:, None])
    return jnp.sum(same.astype(jnp.int32), axis=-1)


def shards(
    sign_iterate,
    sign_square,
    pattern_x,
    pattern_y,
    pattern_product,
    orbital_energy,
    pair_dest,
    pair_block,
    force_h,
    force_s,
):
    rows_x, cols_x = sign_iterate.shape
    xmask = masked_tile(sign_iterate, pattern_x)
    ymask = masked_tile(sign_square, pattern_y)
    y_whole = lax.all_gather(ymask, "row", axis=0, tiled=True)
    product = jnp.dot(
        lax.all_gather(xmask, "col", axis=1, tiled=True),
        y_whole,
        preferred_element_type=jnp.float32,
    )
    product = masked_tile(product, pattern_product)
    xnew = 1.5 * xmask.astype(jnp.float32) - 0.5 * product
    sign_next = xnew.astype(jnp.bfloat16)
    global_rows = lax.axis_index("row") * rows_x + jnp.arange(rows_x, dtype=jnp.int32)
    global_cols = lax.axis_index("col") * cols_x + jnp.arange(cols_x, dtype=jnp.int32)
    identity = (global_rows[:, None] == global_cols[None, :]).astype(jnp.float32)
    density = (0.5 * identity - 0.5 * xnew).astype(jnp.bfloat16)
    dens_blocks = tile_blocks(density)
    n_rows = lax.axis_size("row")
    n_cols = lax.axis_size("col")
    devices = n_rows * n_cols
    slots = devices * CAP
    local_rows = rows_x // BS
    dest = pair_dest[0, :, 0]
    wanted = pair_block[0]
    rank = rank_within(dest)
    slot = dest * CAP + rank
    pick_slot = (jnp.arange(slots, dtype=jnp.int32)[:, None] == slot[None, :]).astype(jnp.bfloat16)
    pick_block = (
        wanted[:, None] == jnp.arange(dens_blocks.shape[0], dtype=jnp.int32)[None, :]
    ).astype(jnp.bfloat16)
    routing_table = jnp.dot(pick_slot, pick_block, preferred_element_type=jnp.float32).astype(
        jnp.bfloat16
    )
    send_dens = jnp.dot(routing_table, dens_blocks, preferred_element_type=jnp.float32).astype(
        jnp.bfloat16
    )
    pick_row = ((wanted // QB)[:, None] == jnp.arange(local_rows, dtype=jnp.int32)[None, :]).astype(
        jnp.bfloat16
    )
    slot_rows = jnp.dot(pick_slot, pick_row, preferred_element_type=jnp.float32).astype(
        jnp.bfloat16
    )
    send_energy = jnp.dot(
        slot_rows, orbital_energy.reshape(local_rows, BS), preferred_element_type=jnp.float32
    ).astype(jnp.bfloat16)
    payload = jnp.concatenate([send_dens.reshape(slots, BS, BS), send_energy[:, None, :]], axis=1)
    height = BS + 1
    received = lax.all_to_all(
        payload.reshape(devices, CAP, height * BS),
        ("row", "col"),
        split_axis=0,
        concat_axis=0,
        tiled=True,
    )
    received = received.reshape(slots, height, BS)
    recv_dens = received[:, :BS, :]
    energies = received[:, BS, :].astype(jnp.float32)
    h_term = jnp.einsum("sab,sab->s", recv_dens, force_h, preferred_element_type=jnp.float32)
    s_rows = jnp.einsum("sab,sab->sa", recv_dens, force_s, preferred_element_type=jnp.float32)
    forces = h_term - jnp.sum(energies * s_rows, axis=1)
    return (sign_next, forces)


ROWS = 4
COLS = 8
DEVICES = ROWS * COLS
LINE = 4
CHUNKS = 4
STEP = 256
HALF = 512


def kernel(
    pat,
    table,
    energy,
    x_hbm,
    y_hbm,
    h_hbm,
    s_hbm,
    sign_hbm,
    parts,
    xg,
    yg,
    acc,
    dens,
    sgn,
    hbuf,
    sbuf,
    wbuf,
    outbox,
    inbox,
    e_out,
    e_in,
    local_sem,
    up_sem,
    down_sem,
    twin_sem,
    x_sem,
    ysend_sem,
    y_sem,
    e_sem,
    esend_sem,
    d_sem,
    dsend_sem,
):
    r = lax.axis_index("row")
    c = lax.axis_index("col")
    me = r * COLS + c
    z = c // 2
    core = c % 2
    row_x = r + 1 - 2 * (r % 2)
    row_y = (r + 2) % 4

    barrier = pltpu.get_barrier_semaphore()

    def greet(i, carry):
        other = (me + i) % DEVICES
        pl.semaphore_signal(
            barrier, inc=1, device_id=(other // COLS, other % COLS), device_id_type=MESH
        )
        return carry

    lax.fori_loop(1, DEVICES, greet, 0)

    get_x = pltpu.make_async_copy(x_hbm, xg.at[c], local_sem.at[0])
    get_y = pltpu.make_async_copy(y_hbm, yg.at[r], local_sem.at[1])
    get_h = pltpu.make_async_copy(h_hbm, hbuf, local_sem.at[2])
    get_s = pltpu.make_async_copy(s_hbm, sbuf, local_sem.at[3])
    get_x.start()
    get_y.start()
    get_h.start()
    get_s.start()

    def mask(ref, slot, base, ch):
        for i in range(STEP // BS):
            rows = pl.ds(ch * STEP + i * BS, BS)
            for j in range(QB):
                keep = pat[base + j, ch * (STEP // BS) + i].astype(jnp.float32)
                block = ref[slot, rows, j * BS : (j + 1) * BS].astype(jnp.float32)
                ref[slot, rows, j * BS : (j + 1) * BS] = (block * keep).astype(jnp.bfloat16)

    def x_copy(panel, ch, where, send_sem):
        block = xg.at[panel, pl.ds(ch * STEP, STEP)]
        return pltpu.make_async_remote_copy(
            src_ref=block,
            dst_ref=block,
            send_sem=send_sem.at[panel // 2, ch],
            recv_sem=x_sem.at[panel, ch],
            device_id=(r, where),
            device_id_type=MESH,
        )

    def up(panel, ch):
        return x_copy(panel, ch, c + 2, up_sem)

    def down(panel, ch):
        return x_copy(panel, ch, c - 2, down_sem)

    def twin(panel, ch):
        return x_copy(panel, ch, c + 1 - 2 * core, twin_sem)

    def y_copy(owner, half, to, number):
        block = yg.at[owner, pl.ds(half * HALF, HALF)]
        return pltpu.make_async_remote_copy(
            src_ref=block,
            dst_ref=block,
            send_sem=ysend_sem.at[number],
            recv_sem=y_sem.at[owner, half],
            device_id=(to, c),
            device_id_type=MESH,
        )

    get_x.wait()
    mask(xg, c, 0, 0)
    pl.semaphore_wait(barrier, DEVICES - 1)

    def send_x(ch):
        @pl.when(z < LINE - 1)
        def _():
            up(c, ch).start()

        @pl.when(z > 0)
        def _():
            down(c, ch).start()

        twin(c, ch).start()

    send_x(0)
    get_y.wait()

    def mask_y(ch, carry):
        mask(yg, r, QB, ch)
        return carry

    lax.fori_loop(0, CHUNKS, mask_y, 0)
    y_copy(r, 0, row_x, 0).start()
    y_copy(r, 1, row_y, 1).start()
    y_copy(r, 1, row_x, 2).start()
    y_copy(r, 0, row_y, 3).start()

    def start_x(ch, carry):
        mask(xg, c, 0, ch)
        send_x(ch)
        return carry

    lax.fori_loop(1, CHUNKS, start_x, 0)

    def pack_energy(o, carry):
        for k in range(CAP):
            e_out[o, k : k + 1, :] = energy[pl.ds(table[0, o * CAP + k] // QB, 1), :]
        for k in range(CAP, 8):
            e_out[o, k : k + 1, :] = jnp.zeros((1, BS), jnp.float32)
        return carry

    lax.fori_loop(0, DEVICES, pack_energy, 0)

    def e_copy(o):
        return pltpu.make_async_remote_copy(
            src_ref=e_out.at[o],
            dst_ref=e_in.at[me],
            send_sem=esend_sem,
            recv_sem=e_sem,
            device_id=(o // COLS, o % COLS),
            device_id_type=MESH,
        )

    def send_energy(i, carry):
        e_copy((me + i) % DEVICES).start()
        return carry

    lax.fori_loop(1, DEVICES, send_energy, 0)
    pltpu.make_async_copy(e_out.at[me], e_in.at[me], e_sem).start()

    dens[QB * 8] = jnp.zeros((BS, BS), jnp.bfloat16)
    get_h.wait()
    get_s.wait()
    pltpu.make_async_copy(e_in, e_in, e_sem).wait()

    eye = lax.broadcasted_iota(jnp.int32, (BS, BS), 0) == lax.broadcasted_iota(
        jnp.int32, (BS, BS), 1
    )

    def weigh(src, carry):
        for k in range(CAP):
            line = jnp.broadcast_to(e_in[src, k : k + 1, :], (BS, BS))
            col = jnp.sum(jnp.where(eye, line, 0.0), axis=1, keepdims=True)
            s = src * CAP + k
            wbuf[s] = hbuf[s].astype(jnp.float32) - col * sbuf[s].astype(jnp.float32)
        return carry

    lax.fori_loop(0, DEVICES, weigh, 0)

    def pass_on(d, ch):
        @pl.when(z >= d)
        def _():
            panel = c - 2 * d
            x_copy(panel, ch, c, up_sem).wait_recv()

            @pl.when(z < LINE - 1)
            def _():
                up(panel, ch).start()

            twin(panel, ch).start()

        @pl.when(z + d < LINE)
        def _():
            panel = c + 2 * d
            x_copy(panel, ch, c, down_sem).wait_recv()

            @pl.when(z > 0)
            def _():
                down(panel, ch).start()

            twin(panel, ch).start()

    def wait_twin(zp, ch):
        x_copy(2 * zp + 1 - core, ch, c, twin_sem).wait_recv()

    def multiply(zp, ch):
        rows = pl.ds(ch * STEP, STEP)
        return jnp.dot(
            xg[2 * zp, rows, :], yg[zp, 0:HALF, :], preferred_element_type=jnp.float32
        ) + jnp.dot(
            xg[2 * zp + 1, rows, :], yg[zp, HALF : 2 * HALF, :], preferred_element_type=jnp.float32
        )

    def add(d, ch):
        rows = pl.ds(ch * STEP, STEP)

        @pl.when(z >= d)
        def _():
            wait_twin(z - d, ch)
            acc[rows, :] += multiply(z - d, ch)

        @pl.when(z + d < LINE)
        def _():
            wait_twin(z + d, ch)
            acc[rows, :] += multiply(z + d, ch)

    def loop(lo, hi, body):
        def step(i, carry):
            body(i)
            return carry

        lax.fori_loop(lo, hi, step, 0)

    loop(0, 2, lambda ch: pass_on(1, ch))
    y_copy(row_x, 0, r, 0).wait_recv()
    y_copy(row_x, 0, row_y, 4).start()
    y_copy(row_y, 1, r, 1).wait_recv()
    y_copy(row_y, 1, row_x, 5).start()
    loop(2, CHUNKS, lambda ch: pass_on(1, ch))
    loop(0, 2, lambda ch: pass_on(2, ch))
    y_copy(row_x, 1, r, 2).wait_recv()
    y_copy(row_y, 0, r, 3).wait_recv()
    row_d = 3 - r
    y_copy(row_d, 0, r, 4).wait_recv()
    y_copy(row_d, 1, r, 5).wait_recv()

    def first(ch):
        wait_twin(z, ch)
        acc[pl.ds(ch * STEP, STEP), :] = multiply(z, ch)

    loop(0, CHUNKS, first)
    loop(0, CHUNKS, lambda ch: add(1, ch))
    loop(2, CHUNKS, lambda ch: pass_on(2, ch))
    loop(0, CHUNKS, lambda ch: add(2, ch))

    eye_f = eye.astype(jnp.float32)

    def finish(ch):
        for i in range(STEP // BS):
            block_row = ch * (STEP // BS) + i
            rows = pl.ds(ch * STEP + i * BS, BS)
            for j in range(QB):
                cols = slice(j * BS, (j + 1) * BS)
                keep = pat[2 * QB + j, block_row].astype(jnp.float32)
                xnew = 1.5 * xg[c, rows, cols].astype(jnp.float32) - 0.5 * (acc[rows, cols] * keep)
                sgn[rows, cols] = xnew.astype(jnp.bfloat16)
                on = jnp.where(r * 8 + block_row == c * QB + j, 0.5, 0.0).astype(jnp.float32)
                dens[block_row * QB + j] = (on * eye_f - 0.5 * xnew).astype(jnp.bfloat16)

    pass_on(3, 0)

    def last(ch):
        pass_on(3, ch)
        add(3, ch - 1)
        finish(ch - 1)

    loop(1, CHUNKS, last)
    add(3, CHUNKS - 1)
    finish(CHUNKS - 1)

    put = pltpu.make_async_copy(sgn, sign_hbm, local_sem.at[4])
    put.start()

    def d_copy(o, src):
        return pltpu.make_async_remote_copy(
            src_ref=outbox.at[o],
            dst_ref=inbox.at[src],
            send_sem=dsend_sem,
            recv_sem=d_sem.at[src],
            device_id=(o // COLS, o % COLS),
            device_id_type=MESH,
        )

    flips = (3 - z, (z + 2) % LINE, z + 1 - 2 * (z % 2), z)
    for n, zz in enumerate(flips):

        def send(j, zz=zz):
            o = (r + j // 2) % ROWS * COLS + zz * 2 + (core + j) % 2
            for k in range(CAP):
                outbox[o, k] = dens[table[0, o * CAP + k]]
            d_copy(o, me).start()

        loop(0 if n < 3 else 1, COLS, send)

    def force(s, block):
        parts[pl.ds(s, 1), :] = jnp.sum(block.astype(jnp.float32) * wbuf[s], axis=0, keepdims=True)

    for k in range(CAP):
        force(me * CAP + k, dens[table[0, me * CAP + k]])

    for n in (3, 2, 1, 0):

        def take(j, zz=flips[n]):
            src = (r + ROWS - j // 2) % ROWS * COLS + zz * 2 + (core + j) % 2
            d_copy(src, src).wait_recv()
            for k in range(CAP):
                force(src * CAP + k, inbox[src, k])

        loop(0 if n < 3 else 1, COLS, take)

    def sent(ch):
        for zp in range(LINE):
            panel = 2 * zp + core

            @pl.when((z >= zp) & (z < LINE - 1))
            def _():
                up(panel, ch).wait_send()

            @pl.when((z <= zp) & (z > 0))
            def _():
                down(panel, ch).wait_send()

            twin(panel, ch).wait_send()

    loop(0, CHUNKS, sent)
    y_copy(r, 0, row_x, 0).wait_send()
    y_copy(r, 1, row_y, 1).wait_send()
    y_copy(r, 1, row_x, 2).wait_send()
    y_copy(r, 0, row_y, 3).wait_send()
    y_copy(row_x, 0, row_y, 4).wait_send()
    y_copy(row_y, 1, row_x, 5).wait_send()
    out = e_out.at[pl.ds(0, DEVICES - 1)]
    pltpu.make_async_copy(out, out, esend_sem).wait()
    out = outbox.at[pl.ds(0, DEVICES - 1)]
    pltpu.make_async_copy(out, out, dsend_sem).wait()
    put.wait()


def fused(
    sign_iterate,
    sign_square,
    pattern_x,
    pattern_y,
    pattern_product,
    orbital_energy,
    pair_dest,
    pair_block,
    force_h,
    force_s,
):
    slots = DEVICES * CAP
    dest = pair_dest[0, :, 0]
    slot = dest * CAP + rank_within(dest)
    none = sign_iterate.shape[0] // BS * QB
    named = slot[:, None] == jnp.arange(slots, dtype=jnp.int32)[None, :]
    table = none - jnp.sum(
        jnp.where(named, none - pair_block[0][:, None], 0), axis=0, keepdims=True
    )
    pat = jnp.concatenate([pattern_x.T, pattern_y.T, pattern_product.T], axis=0)
    energy = orbital_energy.reshape(-1, BS).astype(jnp.float32)
    energy = jnp.concatenate([energy, jnp.zeros_like(energy)], axis=0)
    vmem = pl.BlockSpec(memory_space=pltpu.VMEM)
    smem = pl.BlockSpec(memory_space=pltpu.SMEM)
    hbm = pl.BlockSpec(memory_space=pl.ANY)
    bf16, f32 = jnp.bfloat16, jnp.float32
    dma = pltpu.SemaphoreType.DMA
    sign_next, parts = pl.pallas_call(
        kernel,
        out_shape=(
            jax.ShapeDtypeStruct(sign_iterate.shape, bf16),
            jax.ShapeDtypeStruct((slots, BS), f32),
        ),
        in_specs=[smem, smem, vmem, hbm, hbm, hbm, hbm],
        out_specs=(hbm, vmem),
        scratch_shapes=[
            pltpu.VMEM((COLS, 1024, 512), bf16),
            pltpu.VMEM((ROWS, 1024, 512), bf16),
            pltpu.VMEM((1024, 512), f32),
            pltpu.VMEM((none + 1, BS, BS), bf16),
            pltpu.VMEM((1024, 512), bf16),
            pltpu.VMEM((slots, BS, BS), bf16),
            pltpu.VMEM((slots, BS, BS), bf16),
            pltpu.VMEM((slots, BS, BS), f32),
            pltpu.VMEM((DEVICES, CAP, BS, BS), bf16),
            pltpu.VMEM((DEVICES, CAP, BS, BS), bf16),
            pltpu.VMEM((DEVICES, 8, BS), f32),
            pltpu.VMEM((DEVICES, 8, BS), f32),
            dma((5,)),
            dma((LINE, CHUNKS)),
            dma((LINE, CHUNKS)),
            dma((LINE, CHUNKS)),
            dma((COLS, CHUNKS)),
            dma((6,)),
            dma((ROWS, 2)),
            dma,
            dma,
            dma((DEVICES,)),
            dma,
        ],
        compiler_params=pltpu.CompilerParams(
            collective_id=0, has_side_effects=True, vmem_limit_bytes=48 * 1024 * 1024
        ),
        cost_estimate=pl.CostEstimate(
            flops=2 * 1024 * 4096 * 512, bytes_accessed=8 * 1024 * 1024, transcendentals=0
        ),
    )(pat, table, energy, sign_iterate, sign_square, force_h, force_s)
    return sign_next, jnp.sum(parts, axis=1)


def solution(mesh):
    in_specs = (
        P("row", "col"),
        P("row", "col"),
        P("row", "col"),
        P("row", "col"),
        P("row", "col"),
        P("row"),
        P(("row", "col"), None, None),
        P(("row", "col"), None),
        P(("row", "col"), None, None),
        P(("row", "col"), None, None),
    )
    out_specs = (P("row", "col"), P(("row", "col")))
    body = fused if (mesh.shape["row"], mesh.shape["col"]) == (ROWS, COLS) else shards
    return jax.shard_map(body, mesh=mesh, in_specs=in_specs, out_specs=out_specs, check_vma=False)
```

```python
import functools

import jax
import jax.numpy as jnp
from jax import lax
from jax.experimental import pallas as pl
from jax.experimental.pallas import tpu as pltpu
from jax.sharding import PartitionSpec as P

BS = 128
QB = 4
CAP = 2
MESH = pl.DeviceIdType.MESH


def masked_tile(tile, pattern):
    rows, cols = tile.shape
    shaped = tile.reshape(rows // BS, BS, cols // BS, BS) * pattern[:, None, :, None].astype(
        tile.dtype
    )
    return shaped.reshape(rows, cols)


def tile_blocks(tile):
    rows, cols = tile.shape
    shaped = tile.reshape(rows // BS, BS, cols // BS, BS).transpose(0, 2, 1, 3)
    return shaped.reshape(rows // BS * (cols // BS), BS * BS)


def rank_within(dest):
    entries = dest.shape[-1]
    order = jnp.arange(entries, dtype=jnp.int32)
    same = (dest[..., :, None] == dest[..., None, :]) & (order[None, :] < order[:, None])
    return jnp.sum(same.astype(jnp.int32), axis=-1)


def shards(
    sign_iterate,
    sign_square,
    pattern_x,
    pattern_y,
    pattern_product,
    orbital_energy,
    pair_dest,
    pair_block,
    force_h,
    force_s,
):
    rows_x, cols_x = sign_iterate.shape
    xmask = masked_tile(sign_iterate, pattern_x)
    ymask = masked_tile(sign_square, pattern_y)
    y_whole = lax.all_gather(ymask, "row", axis=0, tiled=True)
    product = jnp.dot(
        lax.all_gather(xmask, "col", axis=1, tiled=True),
        y_whole,
        preferred_element_type=jnp.float32,
    )
    product = masked_tile(product, pattern_product)
    xnew = 1.5 * xmask.astype(jnp.float32) - 0.5 * product
    sign_next = xnew.astype(jnp.bfloat16)
    global_rows = lax.axis_index("row") * rows_x + jnp.arange(rows_x, dtype=jnp.int32)
    global_cols = lax.axis_index("col") * cols_x + jnp.arange(cols_x, dtype=jnp.int32)
    identity = (global_rows[:, None] == global_cols[None, :]).astype(jnp.float32)
    density = (0.5 * identity - 0.5 * xnew).astype(jnp.bfloat16)
    dens_blocks = tile_blocks(density)
    n_rows = lax.axis_size("row")
    n_cols = lax.axis_size("col")
    devices = n_rows * n_cols
    slots = devices * CAP
    local_rows = rows_x // BS
    dest = pair_dest[0, :, 0]
    wanted = pair_block[0]
    rank = rank_within(dest)
    slot = dest * CAP + rank
    pick_slot = (jnp.arange(slots, dtype=jnp.int32)[:, None] == slot[None, :]).astype(jnp.bfloat16)
    pick_block = (
        wanted[:, None] == jnp.arange(dens_blocks.shape[0], dtype=jnp.int32)[None, :]
    ).astype(jnp.bfloat16)
    routing_table = jnp.dot(pick_slot, pick_block, preferred_element_type=jnp.float32).astype(
        jnp.bfloat16
    )
    send_dens = jnp.dot(routing_table, dens_blocks, preferred_element_type=jnp.float32).astype(
        jnp.bfloat16
    )
    pick_row = ((wanted // QB)[:, None] == jnp.arange(local_rows, dtype=jnp.int32)[None, :]).astype(
        jnp.bfloat16
    )
    slot_rows = jnp.dot(pick_slot, pick_row, preferred_element_type=jnp.float32).astype(
        jnp.bfloat16
    )
    send_energy = jnp.dot(
        slot_rows, orbital_energy.reshape(local_rows, BS), preferred_element_type=jnp.float32
    ).astype(jnp.bfloat16)
    payload = jnp.concatenate([send_dens.reshape(slots, BS, BS), send_energy[:, None, :]], axis=1)
    height = BS + 1
    received = lax.all_to_all(
        payload.reshape(devices, CAP, height * BS),
        ("row", "col"),
        split_axis=0,
        concat_axis=0,
        tiled=True,
    )
    received = received.reshape(slots, height, BS)
    recv_dens = received[:, :BS, :]
    energies = received[:, BS, :].astype(jnp.float32)
    h_term = jnp.einsum("sab,sab->s", recv_dens, force_h, preferred_element_type=jnp.float32)
    s_rows = jnp.einsum("sab,sab->sa", recv_dens, force_s, preferred_element_type=jnp.float32)
    forces = h_term - jnp.sum(energies * s_rows, axis=1)
    return (sign_next, forces)


ROWS = 4
COLS = 8
DEVICES = ROWS * COLS
LINE = 4
CHUNKS = 4
TALL = 8
STEP = 256
HALF = 512


def kernel(
    room,
    pat_x,
    pat_y,
    pat_p,
    dest,
    wanted,
    pat_tile,
    energy,
    x_hbm,
    y_hbm,
    h_hbm,
    s_hbm,
    sign_hbm,
    parts,
    xraw,
    lines,
    twins,
    xg,
    yg,
    acc,
    dens,
    sgn,
    hbuf,
    sbuf,
    wbuf,
    outbox,
    inbox,
    e_out,
    e_in,
    e_rows,
    t_out,
    t_in,
    pats,
    ahead,
    listed,
    place,
    table,
    local_sem,
    up_sem,
    down_sem,
    twin_sem,
    x_sem,
    tx_sem,
    ysend_sem,
    y_sem,
    e_sem,
    esend_sem,
    d_sem,
    dsend_sem,
    t_sem,
    tsend_sem,
):
    chunk = room // CHUNKS
    r = lax.axis_index("row")
    c = lax.axis_index("col")
    me = r * COLS + c
    z = c // 2
    core = c % 2
    row_x = r + 1 - 2 * (r % 2)
    row_y = (r + 2) % 4

    barrier = pltpu.get_barrier_semaphore()

    def greet(i, carry):
        other = (me + i) % DEVICES
        pl.semaphore_signal(
            barrier, inc=1, device_id=(other // COLS, other % COLS), device_id_type=MESH
        )
        return carry

    lax.fori_loop(1, DEVICES, greet, 0)

    for j in range(QB):
        pltpu.make_async_copy(
            x_hbm.at[:, :, j * BS : (j + 1) * BS],
            xraw.at[pl.ds(j * TALL, TALL)],
            local_sem.at[0],
        ).start()
    get_x = pltpu.make_async_copy(xraw, xraw, local_sem.at[0])
    get_y = pltpu.make_async_copy(y_hbm, yg.at[r], local_sem.at[1])
    get_h = pltpu.make_async_copy(h_hbm, hbuf, local_sem.at[2])
    get_s = pltpu.make_async_copy(s_hbm, sbuf, local_sem.at[3])
    get_y.start()
    get_h.start()
    get_s.start()

    def loop(lo, hi, body):
        def step(i, carry):
            body(i)
            return carry

        lax.fori_loop(lo, hi, step, 0)

    def x_copy(src, dst, ch, col, send_sem, recv_sem):
        rows = pl.ds(ch * chunk, chunk)
        return pltpu.make_async_remote_copy(
            src_ref=src.at[rows],
            dst_ref=dst.at[rows],
            send_sem=send_sem,
            recv_sem=recv_sem,
            device_id=(r, col),
            device_id_type=MESH,
        )

    def up(d, ch):
        return x_copy(lines[d], lines[d + 1], ch, c + 2, up_sem.at[d, ch], x_sem.at[d + 1, ch])

    def down(d, ch):
        src = lines[d + LINE - 1] if d else lines[0]
        to = d + LINE
        return x_copy(src, lines[to], ch, c - 2, down_sem.at[d, ch], x_sem.at[to, ch])

    def twin(i, ch):
        other = c + 1 - 2 * core
        return x_copy(lines[i], twins[i], ch, other, twin_sem.at[i, ch], tx_sem.at[i, ch])

    def y_copy(owner, half, to, number):
        block = yg.at[owner, pl.ds(half * HALF, HALF)]
        return pltpu.make_async_remote_copy(
            src_ref=block,
            dst_ref=block,
            send_sem=ysend_sem.at[number],
            recv_sem=y_sem.at[owner, half],
            device_id=(to, c),
            device_id_type=MESH,
        )

    t_out[...] = jnp.zeros_like(t_out)
    t_out[0:QB, 0:TALL] = pat_tile[...]
    blocks = QB * TALL
    number = jnp.int32(0)
    spots = []
    for b in range(blocks):
        on = pat_x[b // TALL, b % TALL]
        spots.append(on * number + (1 - on) * blocks)
        number = number + on
    count = number
    for b in range(blocks):
        ahead[b] = spots[b]

    def seek(t):
        found = jnp.int32(0)
        for b in range(blocks):
            found = found + (ahead[b] == t).astype(jnp.int32) * b
        listed[t] = found

    loop(0, room, seek)
    get_x.wait()

    def compact(t):
        lines[0][t] = xraw[listed[t]]

    loop(0, room, compact)
    pl.semaphore_wait(barrier, DEVICES - 1)

    def t_copy(col):
        return pltpu.make_async_remote_copy(
            src_ref=t_out,
            dst_ref=t_in.at[c],
            send_sem=tsend_sem,
            recv_sem=t_sem,
            device_id=(r, col),
            device_id_type=MESH,
        )

    loop(1, COLS, lambda i: t_copy((c + i) % COLS).start())
    pltpu.make_async_copy(t_out, t_in.at[c], t_sem).start()

    def send_x(ch):
        @pl.when(z < LINE - 1)
        def _():
            up(0, ch).start()

        @pl.when(z > 0)
        def _():
            down(0, ch).start()

        twin(0, ch).start()

    loop(0, CHUNKS, send_x)
    get_y.wait()

    def mask_y(i):
        rows = pl.ds(i * BS, BS)
        for j in range(QB):
            cols = slice(j * BS, (j + 1) * BS)
            keep = pat_y[j, i].astype(jnp.float32)
            yg[r, rows, cols] = (yg[r, rows, cols].astype(jnp.float32) * keep).astype(jnp.bfloat16)

    loop(0, TALL, mask_y)
    y_copy(r, 0, row_x, 0).start()
    y_copy(r, 1, row_y, 1).start()
    y_copy(r, 1, row_x, 2).start()
    y_copy(r, 0, row_y, 3).start()

    def mask_x(i):
        rows = pl.ds(i * BS, BS)
        for j in range(QB):
            keep = pat_x[j, i].astype(jnp.float32)
            block = xraw[j * TALL + i].astype(jnp.float32) * keep
            xg[c, rows, j * BS : (j + 1) * BS] = block.astype(jnp.bfloat16)

    loop(0, TALL, mask_x)

    def find(o):
        seen = jnp.int32(0)
        slots = [jnp.int32(blocks)] * CAP
        for p in range(dest.shape[1]):
            hit = (dest[0, p] == o).astype(jnp.int32)
            for k in range(CAP):
                first_seen = hit * (seen == k).astype(jnp.int32)
                slots[k] = slots[k] + first_seen * (wanted[0, p] - blocks)
            seen = seen + hit
        for k in range(CAP):
            table[o * CAP + k] = slots[k]

    loop(0, DEVICES, find)
    e_rows[0:TALL, :] = energy[...].astype(jnp.float32)
    e_rows[TALL : 2 * TALL, :] = jnp.zeros((TALL, BS), jnp.float32)

    def pack_energy(o, carry):
        for k in range(CAP):
            e_out[o, k : k + 1, :] = e_rows[pl.ds(table[o * CAP + k] // QB, 1), :]
        for k in range(CAP, 8):
            e_out[o, k : k + 1, :] = jnp.full((1, BS), count.astype(jnp.float32))
        return carry

    lax.fori_loop(0, DEVICES, pack_energy, 0)

    def e_copy(o):
        return pltpu.make_async_remote_copy(
            src_ref=e_out.at[o],
            dst_ref=e_in.at[me],
            send_sem=esend_sem,
            recv_sem=e_sem,
            device_id=(o // COLS, o % COLS),
            device_id_type=MESH,
        )

    def send_energy(i, carry):
        e_copy((me + i) % DEVICES).start()
        return carry

    lax.fori_loop(1, DEVICES, send_energy, 0)
    pltpu.make_async_copy(e_out.at[me], e_in.at[me], e_sem).start()

    dens[QB * 8] = jnp.zeros((BS, BS), jnp.bfloat16)
    get_h.wait()
    get_s.wait()
    pltpu.make_async_copy(e_in, e_in, e_sem).wait()

    eye = lax.broadcasted_iota(jnp.int32, (BS, BS), 0) == lax.broadcasted_iota(
        jnp.int32, (BS, BS), 1
    )

    def weigh(src, carry):
        for k in range(CAP):
            line = jnp.broadcast_to(e_in[src, k : k + 1, :], (BS, BS))
            col = jnp.sum(jnp.where(eye, line, 0.0), axis=1, keepdims=True)
            s = src * CAP + k
            wbuf[s] = hbuf[s].astype(jnp.float32) - col * sbuf[s].astype(jnp.float32)
        return carry

    lax.fori_loop(0, DEVICES, weigh, 0)

    most = e_in[0]
    for src in range(1, DEVICES):
        most = jnp.maximum(most, e_in[src])
    parts[DEVICES * CAP : DEVICES * CAP + 8, :] = jnp.broadcast_to(most[CAP : CAP + 1, :], (8, BS))

    pltpu.make_async_copy(t_in, t_in, t_sem).wait()
    get_pats = pltpu.make_async_copy(t_in, pats, local_sem.at[5])
    get_pats.start()
    get_pats.wait()

    for ref in (*lines, *twins):
        ref[blocks] = jnp.zeros((BS, BS), jnp.bfloat16)

    def locate(panel):
        number = jnp.int32(0)
        for b in range(blocks):
            on = pats[panel, b // TALL, b % TALL]
            place[panel, b] = on * number + (1 - on) * blocks
            number = number + on

    loop(0, COLS, locate)

    def pass_on(d, ch):
        @pl.when(z >= d)
        def _():
            up(d - 1, ch).wait_recv()
            if d < LINE - 1:

                @pl.when(z < LINE - 1)
                def _():
                    up(d, ch).start()

            twin(d, ch).start()

        @pl.when(z + d < LINE)
        def _():
            down(d - 1, ch).wait_recv()
            if d < LINE - 1:

                @pl.when(z > 0)
                def _():
                    down(d, ch).start()

            twin(LINE - 1 + d, ch).start()

    def wait_twin(i):
        loop(0, CHUNKS, lambda ch: twin(i, ch).wait_recv())

    def expand(ref, panel, ch):
        for i in range(STEP // BS):
            row = ch * (STEP // BS) + i
            for j in range(QB):
                block = ref[place[panel, j * TALL + row]]
                xg[panel, pl.ds(row * BS, BS), j * BS : (j + 1) * BS] = block

    def multiply(zp, ch):
        rows = pl.ds(ch * STEP, STEP)
        return jnp.dot(
            xg[2 * zp, rows, :], yg[zp, 0:HALF, :], preferred_element_type=jnp.float32
        ) + jnp.dot(
            xg[2 * zp + 1, rows, :], yg[zp, HALF : 2 * HALF, :], preferred_element_type=jnp.float32
        )

    def add(d):
        def panels(zp, i):
            wait_twin(i)

            def one(ch):
                expand(lines[i], 2 * zp + core, ch)
                expand(twins[i], 2 * zp + 1 - core, ch)
                acc[pl.ds(ch * STEP, STEP), :] += multiply(zp, ch)

            loop(0, CHUNKS, one)

        @pl.when(z >= d)
        def _():
            panels(z - d, d)

        @pl.when(z + d < LINE)
        def _():
            panels(z + d, LINE - 1 + d)

    loop(0, 2, lambda ch: pass_on(1, ch))
    y_copy(row_x, 0, r, 0).wait_recv()
    y_copy(row_x, 0, row_y, 4).start()
    y_copy(row_y, 1, r, 1).wait_recv()
    y_copy(row_y, 1, row_x, 5).start()
    loop(2, CHUNKS, lambda ch: pass_on(1, ch))
    loop(0, 2, lambda ch: pass_on(2, ch))
    y_copy(row_x, 1, r, 2).wait_recv()
    y_copy(row_y, 0, r, 3).wait_recv()
    row_d = 3 - r
    y_copy(row_d, 0, r, 4).wait_recv()
    y_copy(row_d, 1, r, 5).wait_recv()

    wait_twin(0)

    def first(ch):
        expand(twins[0], 2 * z + 1 - core, ch)
        acc[pl.ds(ch * STEP, STEP), :] = multiply(z, ch)

    loop(0, CHUNKS, first)
    add(1)
    loop(2, CHUNKS, lambda ch: pass_on(2, ch))
    add(2)

    eye_f = eye.astype(jnp.float32)

    def finish(ch):
        for i in range(STEP // BS):
            block_row = ch * (STEP // BS) + i
            rows = pl.ds(ch * STEP + i * BS, BS)
            for j in range(QB):
                cols = slice(j * BS, (j + 1) * BS)
                keep = pat_p[j, block_row].astype(jnp.float32)
                xnew = 1.5 * xg[c, rows, cols].astype(jnp.float32) - 0.5 * (acc[rows, cols] * keep)
                sgn[rows, cols] = xnew.astype(jnp.bfloat16)
                on = jnp.where(r * 8 + block_row == c * QB + j, 0.5, 0.0).astype(jnp.float32)
                dens[block_row * QB + j] = (on * eye_f - 0.5 * xnew).astype(jnp.bfloat16)

    loop(0, CHUNKS, lambda ch: pass_on(3, ch))
    add(3)
    loop(0, CHUNKS, finish)

    put = pltpu.make_async_copy(sgn, sign_hbm, local_sem.at[4])
    put.start()

    def d_copy(o, src):
        return pltpu.make_async_remote_copy(
            src_ref=outbox.at[o],
            dst_ref=inbox.at[src],
            send_sem=dsend_sem,
            recv_sem=d_sem.at[src],
            device_id=(o // COLS, o % COLS),
            device_id_type=MESH,
        )

    inner = z * (LINE - 1 - z) // 2
    near = z + 1 - 2 * (z % 2)
    far = (z + 2) % LINE
    planes = (
        LINE - 1 - z,
        far + inner * (z - far),
        near + inner * (far - near),
        z + inner * (near - z),
    )
    for zz in planes:

        def send(j, zz=zz):
            o = (r + j // 2) % ROWS * COLS + zz * 2 + (core + j) % 2

            @pl.when(o != me)
            def _():
                for k in range(CAP):
                    outbox[o, k] = dens[table[o * CAP + k]]
                d_copy(o, me).start()

        loop(0, COLS, send)

    def force(s, block):
        parts[pl.ds(s, 1), :] = jnp.sum(block.astype(jnp.float32) * wbuf[s], axis=0, keepdims=True)

    for k in range(CAP):
        force(me * CAP + k, dens[table[me * CAP + k]])

    for zz in (1, 2, 0, 3):

        def take(j, zz=zz):
            src = (r + ROWS - j // 2) % ROWS * COLS + zz * 2 + (core + j) % 2

            @pl.when(src != me)
            def _():
                d_copy(src, src).wait_recv()
                for k in range(CAP):
                    force(src * CAP + k, inbox[src, k])

        loop(0, COLS, take)

    def sent(ch):
        twin(0, ch).wait_send()
        for d in range(LINE):

            @pl.when(z >= d)
            def _(d=d):
                if d:
                    twin(d, ch).wait_send()
                if d < LINE - 1:

                    @pl.when(z < LINE - 1)
                    def _():
                        up(d, ch).wait_send()

            @pl.when(z + d < LINE)
            def _(d=d):
                if d:
                    twin(LINE - 1 + d, ch).wait_send()
                if d < LINE - 1:

                    @pl.when(z > 0)
                    def _():
                        down(d, ch).wait_send()

    loop(0, CHUNKS, sent)
    y_copy(r, 0, row_x, 0).wait_send()
    y_copy(r, 1, row_y, 1).wait_send()
    y_copy(r, 1, row_x, 2).wait_send()
    y_copy(r, 0, row_y, 3).wait_send()
    y_copy(row_x, 0, row_y, 4).wait_send()
    y_copy(row_y, 1, row_x, 5).wait_send()
    out = t_in.at[pl.ds(0, COLS - 1)]
    pltpu.make_async_copy(out, out, tsend_sem).wait()
    out = e_out.at[pl.ds(0, DEVICES - 1)]
    pltpu.make_async_copy(out, out, esend_sem).wait()
    out = outbox.at[pl.ds(0, DEVICES - 1)]
    pltpu.make_async_copy(out, out, dsend_sem).wait()
    put.wait()


def fused(
    room,
    number,
    sign_iterate,
    sign_square,
    pattern_x,
    pattern_y,
    pattern_product,
    orbital_energy,
    pair_dest,
    pair_block,
    force_h,
    force_s,
):
    slots = DEVICES * CAP
    blocks = QB * TALL
    vmem = pl.BlockSpec(memory_space=pltpu.VMEM)
    smem = pl.BlockSpec(memory_space=pltpu.SMEM)
    hbm = pl.BlockSpec(memory_space=pl.ANY)
    bf16, f32, i32 = jnp.bfloat16, jnp.float32, jnp.int32
    dma = pltpu.SemaphoreType.DMA
    tile = sign_iterate.shape
    return pl.pallas_call(
        functools.partial(kernel, room),
        out_shape=(
            jax.ShapeDtypeStruct(tile, bf16),
            jax.ShapeDtypeStruct((slots + 8, BS), f32),
        ),
        in_specs=[smem] * 5 + [vmem] * 2 + [hbm] * 4,
        out_specs=(hbm, vmem),
        scratch_shapes=[
            pltpu.VMEM((blocks, BS, BS), bf16),
            [pltpu.VMEM((blocks + 1, BS, BS), bf16)] * (2 * LINE - 1),
            [pltpu.VMEM((blocks + 1, BS, BS), bf16)] * (2 * LINE - 1),
            pltpu.VMEM((COLS, *tile), bf16),
            pltpu.VMEM((ROWS, *tile), bf16),
            pltpu.VMEM(tile, f32),
            pltpu.VMEM((blocks + 1, BS, BS), bf16),
            pltpu.VMEM(tile, bf16),
            pltpu.VMEM((slots, BS, BS), bf16),
            pltpu.VMEM((slots, BS, BS), bf16),
            pltpu.VMEM((slots, BS, BS), f32),
            pltpu.VMEM((DEVICES, CAP, BS, BS), bf16),
            pltpu.VMEM((DEVICES, CAP, BS, BS), bf16),
            pltpu.VMEM((DEVICES, 8, BS), f32),
            pltpu.VMEM((DEVICES, 8, BS), f32),
            pltpu.VMEM((2 * TALL, BS), f32),
            pltpu.VMEM((8, BS), i32),
            pltpu.VMEM((COLS, 8, BS), i32),
            pltpu.SMEM((COLS, 8, BS), i32),
            pltpu.SMEM((blocks,), i32),
            pltpu.SMEM((blocks,), i32),
            pltpu.SMEM((COLS, blocks), i32),
            pltpu.SMEM((slots,), i32),
            dma((6,)),
            dma((LINE - 1, CHUNKS)),
            dma((LINE - 1, CHUNKS)),
            dma((2 * LINE - 1, CHUNKS)),
            dma((2 * LINE - 1, CHUNKS)),
            dma((2 * LINE - 1, CHUNKS)),
            dma((6,)),
            dma((ROWS, 2)),
            dma,
            dma,
            dma((DEVICES,)),
            dma,
            dma,
            dma,
        ],
        compiler_params=pltpu.CompilerParams(
            collective_id=number, has_side_effects=True, vmem_limit_bytes=60 * 1024 * 1024
        ),
        cost_estimate=pl.CostEstimate(
            flops=2 * 1024 * 4096 * 512, bytes_accessed=8 * 1024 * 1024, transcendentals=0
        ),
        name=f"room_{room}",
    )(
        pattern_x.T,
        pattern_y.T,
        pattern_product.T,
        pair_dest[:, :, 0],
        pair_block,
        pattern_x.T,
        orbital_energy.reshape(-1, BS),
        sign_iterate.reshape(TALL, BS, tile[1]),
        sign_square,
        force_h,
        force_s,
    )


ROOM = 24


def adaptive(*arrays):
    sign_next, parts = fused(ROOM, 0, *arrays)
    short = parts[DEVICES * CAP, 0] > ROOM
    sign_next, parts = lax.cond(
        short, lambda: tuple(fused(QB * TALL, 1, *arrays)), lambda: (sign_next, parts)
    )
    return sign_next, jnp.sum(parts[: DEVICES * CAP], axis=1)


def solution(mesh):
    in_specs = (
        P("row", "col"),
        P("row", "col"),
        P("row", "col"),
        P("row", "col"),
        P("row", "col"),
        P("row"),
        P(("row", "col"), None, None),
        P(("row", "col"), None),
        P(("row", "col"), None, None),
        P(("row", "col"), None, None),
    )
    out_specs = (P("row", "col"), P(("row", "col")))
    body = adaptive if (mesh.shape["row"], mesh.shape["col"]) == (ROWS, COLS) else shards
    return jax.shard_map(body, mesh=mesh, in_specs=in_specs, out_specs=out_specs, check_vma=False)
```

```python
import functools

import jax
import jax.numpy as jnp
from jax import lax
from jax.experimental import pallas as pl
from jax.experimental.pallas import tpu as pltpu
from jax.sharding import PartitionSpec as P

BS = 128
QB = 4
CAP = 2
MESH = pl.DeviceIdType.MESH


def masked_tile(tile, pattern):
    rows, cols = tile.shape
    shaped = tile.reshape(rows // BS, BS, cols // BS, BS) * pattern[:, None, :, None].astype(
        tile.dtype
    )
    return shaped.reshape(rows, cols)


def tile_blocks(tile):
    rows, cols = tile.shape
    shaped = tile.reshape(rows // BS, BS, cols // BS, BS).transpose(0, 2, 1, 3)
    return shaped.reshape(rows // BS * (cols // BS), BS * BS)


def rank_within(dest):
    entries = dest.shape[-1]
    order = jnp.arange(entries, dtype=jnp.int32)
    same = (dest[..., :, None] == dest[..., None, :]) & (order[None, :] < order[:, None])
    return jnp.sum(same.astype(jnp.int32), axis=-1)


def shards(
    sign_iterate,
    sign_square,
    pattern_x,
    pattern_y,
    pattern_product,
    orbital_energy,
    pair_dest,
    pair_block,
    force_h,
    force_s,
):
    rows_x, cols_x = sign_iterate.shape
    xmask = masked_tile(sign_iterate, pattern_x)
    ymask = masked_tile(sign_square, pattern_y)
    y_whole = lax.all_gather(ymask, "row", axis=0, tiled=True)
    product = jnp.dot(
        lax.all_gather(xmask, "col", axis=1, tiled=True),
        y_whole,
        preferred_element_type=jnp.float32,
    )
    product = masked_tile(product, pattern_product)
    xnew = 1.5 * xmask.astype(jnp.float32) - 0.5 * product
    sign_next = xnew.astype(jnp.bfloat16)
    global_rows = lax.axis_index("row") * rows_x + jnp.arange(rows_x, dtype=jnp.int32)
    global_cols = lax.axis_index("col") * cols_x + jnp.arange(cols_x, dtype=jnp.int32)
    identity = (global_rows[:, None] == global_cols[None, :]).astype(jnp.float32)
    density = (0.5 * identity - 0.5 * xnew).astype(jnp.bfloat16)
    dens_blocks = tile_blocks(density)
    n_rows = lax.axis_size("row")
    n_cols = lax.axis_size("col")
    devices = n_rows * n_cols
    slots = devices * CAP
    local_rows = rows_x // BS
    dest = pair_dest[0, :, 0]
    wanted = pair_block[0]
    rank = rank_within(dest)
    slot = dest * CAP + rank
    pick_slot = (jnp.arange(slots, dtype=jnp.int32)[:, None] == slot[None, :]).astype(jnp.bfloat16)
    pick_block = (
        wanted[:, None] == jnp.arange(dens_blocks.shape[0], dtype=jnp.int32)[None, :]
    ).astype(jnp.bfloat16)
    routing_table = jnp.dot(pick_slot, pick_block, preferred_element_type=jnp.float32).astype(
        jnp.bfloat16
    )
    send_dens = jnp.dot(routing_table, dens_blocks, preferred_element_type=jnp.float32).astype(
        jnp.bfloat16
    )
    pick_row = ((wanted // QB)[:, None] == jnp.arange(local_rows, dtype=jnp.int32)[None, :]).astype(
        jnp.bfloat16
    )
    slot_rows = jnp.dot(pick_slot, pick_row, preferred_element_type=jnp.float32).astype(
        jnp.bfloat16
    )
    send_energy = jnp.dot(
        slot_rows, orbital_energy.reshape(local_rows, BS), preferred_element_type=jnp.float32
    ).astype(jnp.bfloat16)
    payload = jnp.concatenate([send_dens.reshape(slots, BS, BS), send_energy[:, None, :]], axis=1)
    height = BS + 1
    received = lax.all_to_all(
        payload.reshape(devices, CAP, height * BS),
        ("row", "col"),
        split_axis=0,
        concat_axis=0,
        tiled=True,
    )
    received = received.reshape(slots, height, BS)
    recv_dens = received[:, :BS, :]
    energies = received[:, BS, :].astype(jnp.float32)
    h_term = jnp.einsum("sab,sab->s", recv_dens, force_h, preferred_element_type=jnp.float32)
    s_rows = jnp.einsum("sab,sab->sa", recv_dens, force_s, preferred_element_type=jnp.float32)
    forces = h_term - jnp.sum(energies * s_rows, axis=1)
    return (sign_next, forces)


ROWS = 4
COLS = 8
DEVICES = ROWS * COLS
LINE = 4
CHUNKS = 4
TALL = 8
STEP = 256
PIECES = 2
KEPT = 16
HALF = 512


def kernel(
    room,
    pat_x,
    pat_y,
    pat_p,
    dest,
    wanted,
    pat_tile,
    energy,
    x_hbm,
    y_hbm,
    h_hbm,
    s_hbm,
    sign_hbm,
    parts,
    short,
    xraw,
    lines,
    spill_out,
    spill_in,
    xg,
    yg,
    acc,
    dens,
    sgn,
    hbuf,
    sbuf,
    wbuf,
    outbox,
    inbox,
    e_out,
    e_in,
    e_table,
    e_rows,
    t_out,
    t_in,
    pats,
    ahead,
    listed,
    place,
    tallies,
    table,
    local_sem,
    up_sem,
    down_sem,
    twin_sem,
    x_sem,
    tx_sem,
    ysend_sem,
    y_sem,
    e_sem,
    esend_sem,
    d_sem,
    dsend_sem,
    t_sem,
    tsend_sem,
    spill_sem,
    rows_sem,
    rsend_sem,
):
    blocks = QB * TALL
    piece = room // PIECES
    spill = blocks - room
    r = lax.axis_index("row")
    c = lax.axis_index("col")
    me = r * COLS + c
    z = c // 2
    core = c % 2
    row_x = r + 1 - 2 * (r % 2)
    row_y = (r + 2) % 4

    barrier = pltpu.get_barrier_semaphore()

    def greet(i, carry):
        other = (me + i) % DEVICES
        pl.semaphore_signal(
            barrier, inc=1, device_id=(other // COLS, other % COLS), device_id_type=MESH
        )
        return carry

    lax.fori_loop(1, DEVICES, greet, 0)

    for j in range(QB):
        pltpu.make_async_copy(
            x_hbm.at[:, :, j * BS : (j + 1) * BS],
            xraw.at[pl.ds(j * TALL, TALL)],
            local_sem.at[0],
        ).start()
    whole = xraw.at[pl.ds(0, blocks)]
    get_x = pltpu.make_async_copy(whole, whole, local_sem.at[0])
    get_y = pltpu.make_async_copy(y_hbm, yg.at[r], local_sem.at[1])
    get_h = pltpu.make_async_copy(h_hbm, hbuf, local_sem.at[2])
    get_s = pltpu.make_async_copy(s_hbm, sbuf, local_sem.at[3])
    get_y.start()
    get_h.start()
    get_s.start()

    def loop(lo, hi, body):
        def step(i, carry):
            body(i)
            return carry

        lax.fori_loop(lo, hi, step, 0)

    half = blocks + 1

    def x_copy(src, dst, ch, col, send_sem, recv_sem):
        rows = pl.ds(core * half + ch * piece, piece)
        return pltpu.make_async_remote_copy(
            src_ref=lines[src].at[rows],
            dst_ref=lines[dst].at[rows],
            send_sem=send_sem,
            recv_sem=recv_sem,
            device_id=(r, col),
            device_id_type=MESH,
        )

    def up(d, ch):
        return x_copy(d, d + 1, ch, c + 2, up_sem.at[d, ch], x_sem.at[d + 1, ch])

    def down(d, ch):
        to = d + LINE
        src = to - 1 if d else 0
        return x_copy(src, to, ch, c - 2, down_sem.at[d, ch], x_sem.at[to, ch])

    twin_col = c + 1 - 2 * core

    def twin(i, ch):
        return x_copy(i, i, ch, twin_col, twin_sem.at[i, ch], tx_sem.at[i, ch])

    def from_twin(i, ch):
        rows = pl.ds((1 - core) * half + ch * piece, piece)
        return pltpu.make_async_copy(lines[i].at[rows], lines[i].at[rows], tx_sem.at[i, ch])

    def y_copy(owner, half, to, number):
        block = yg.at[owner, pl.ds(half * HALF, HALF)]
        return pltpu.make_async_remote_copy(
            src_ref=block,
            dst_ref=block,
            send_sem=ysend_sem.at[number],
            recv_sem=y_sem.at[owner, half],
            device_id=(to, c),
            device_id_type=MESH,
        )

    t_out[...] = jnp.zeros_like(t_out)
    t_out[0:QB, 0:TALL] = pat_tile[...]
    number = jnp.int32(0)
    for b in range(blocks):
        number = number + pat_x[b // TALL, b % TALL]
        ahead[b] = number
    count = number

    def seek(t):
        found = jnp.int32(0)
        for b in range(blocks):
            found = found + (ahead[b] <= t).astype(jnp.int32)
        listed[t] = found

    loop(0, blocks, seek)
    xraw[blocks] = jnp.zeros((BS, BS), jnp.bfloat16)

    def at_least(n, low):
        return low + (n > low).astype(jnp.int32) * (n - low)

    get_x.wait()

    early = KEPT if spill else room

    def compact(t):
        lines[0][core * half + t] = xraw[listed[t]]

    loop(0, early, compact)
    for t in range(spill):
        spill_out[t] = xraw[listed[room + t]]
    if spill:
        spill_in[spill] = jnp.zeros((BS, BS), jnp.bfloat16)
    pl.semaphore_wait(barrier, DEVICES - 1)

    def t_copy(col):
        return pltpu.make_async_remote_copy(
            src_ref=t_out,
            dst_ref=t_in.at[c],
            send_sem=tsend_sem,
            recv_sem=t_sem,
            device_id=(r, col),
            device_id_type=MESH,
        )

    loop(1, COLS, lambda i: t_copy((c + i) % COLS).start())
    pltpu.make_async_copy(t_out, t_in.at[c], t_sem).start()

    def send_x(ch):
        @pl.when(z < LINE - 1)
        def _():
            up(0, ch).start()

        @pl.when(z > 0)
        def _():
            down(0, ch).start()

        twin(0, ch).start()

    hand_over = None
    if spill:
        hand_over = pltpu.make_async_remote_copy(
            src_ref=spill_out,
            dst_ref=spill_in.at[pl.ds(0, spill)],
            send_sem=spill_sem.at[0],
            recv_sem=spill_sem.at[1],
            device_id=(r, twin_col),
            device_id_type=MESH,
        )
        hand_over.start()
    send_x(0)
    if spill:
        hand_over.wait_recv()
        used = at_least(count, KEPT)

        def fill(t):
            own = (t < count).astype(jnp.int32)
            extra = spill_in[own * spill + (1 - own) * (t - used) * (t >= used).astype(jnp.int32)]
            lines[0][core * half + t] = xraw[listed[t]] + extra

        loop(early, room, fill)
    loop(1, PIECES, send_x)
    get_y.wait()

    def mask_y(i):
        rows = pl.ds(i * BS, BS)
        for j in range(QB):
            cols = slice(j * BS, (j + 1) * BS)
            keep = pat_y[j, i].astype(jnp.float32)
            yg[r, rows, cols] = (yg[r, rows, cols].astype(jnp.float32) * keep).astype(jnp.bfloat16)

    loop(0, TALL, mask_y)
    y_copy(r, 0, row_x, 0).start()
    y_copy(r, 1, row_y, 1).start()
    y_copy(r, 1, row_x, 2).start()
    y_copy(r, 0, row_y, 3).start()

    def mask_x(i):
        rows = pl.ds(i * BS, BS)
        for j in range(QB):
            keep = pat_x[j, i].astype(jnp.float32)
            block = xraw[j * TALL + i].astype(jnp.float32) * keep
            xg[c, rows, j * BS : (j + 1) * BS] = block.astype(jnp.bfloat16)

    loop(0, TALL, mask_x)

    def find(o):
        seen = jnp.int32(0)
        slots = [jnp.int32(blocks)] * CAP
        for p in range(dest.shape[1]):
            hit = (dest[0, p] == o).astype(jnp.int32)
            for k in range(CAP):
                first_seen = hit * (seen == k).astype(jnp.int32)
                slots[k] = slots[k] + first_seen * (wanted[0, p] - blocks)
            seen = seen + hit
        for k in range(CAP):
            table[o * CAP + k] = slots[k]

    loop(0, DEVICES, find)
    lanes = lax.broadcasted_iota(jnp.int32, (1, BS), 1)

    def pack(o):
        line = jnp.full((1, BS), count)
        for k in range(CAP):
            line = jnp.where(lanes == k, table[o * CAP + k], line)
        e_out[o] = line

    loop(0, DEVICES, pack)

    def e_copy(o):
        return pltpu.make_async_remote_copy(
            src_ref=e_out.at[o],
            dst_ref=e_in.at[me],
            send_sem=esend_sem,
            recv_sem=e_sem,
            device_id=(o // COLS, o % COLS),
            device_id_type=MESH,
        )

    loop(1, DEVICES, lambda i: e_copy((me + i) % DEVICES).start())
    pltpu.make_async_copy(e_out.at[me], e_in.at[me], e_sem).start()

    for i in range(ROWS):
        e_rows[i, TALL : 2 * TALL, :] = jnp.zeros((TALL, BS), jnp.float32)
    own_rows = e_rows.at[r, pl.ds(0, TALL)]
    own_rows[...] = energy[...].astype(jnp.float32)

    def row_copy(i):
        return pltpu.make_async_remote_copy(
            src_ref=own_rows,
            dst_ref=own_rows,
            send_sem=rsend_sem.at[i],
            recv_sem=rows_sem.at[r],
            device_id=((r + i) % ROWS, c),
            device_id_type=MESH,
        )

    def row_arrival(i):
        other = (r + i) % ROWS
        ref = e_rows.at[other, pl.ds(0, TALL)]
        return pltpu.make_async_copy(ref, ref, rows_sem.at[other])

    for i in range(1, ROWS):
        row_copy(i).start()

    dens[QB * 8] = jnp.zeros((BS, BS), jnp.bfloat16)
    get_h.wait()
    get_s.wait()
    pltpu.make_async_copy(e_in, e_in, e_sem).wait()
    get_table = pltpu.make_async_copy(e_in, e_table, local_sem.at[5])
    get_table.start()
    get_table.wait()
    for i in range(1, ROWS):
        row_arrival(i).wait()

    eye = lax.broadcasted_iota(jnp.int32, (BS, BS), 0) == lax.broadcasted_iota(
        jnp.int32, (BS, BS), 1
    )

    def weigh(src, carry):
        for k in range(CAP):
            line = e_rows[src // COLS, pl.ds(e_table[src, 0, k] // QB, 1), :]
            line = jnp.broadcast_to(line, (BS, BS))
            col = jnp.sum(jnp.where(eye, line, 0.0), axis=1, keepdims=True)
            s = src * CAP + k
            wbuf[s] = hbuf[s].astype(jnp.float32) - col * sbuf[s].astype(jnp.float32)
        return carry

    lax.fori_loop(0, DEVICES, weigh, 0)

    wrong = jnp.int32(0)
    for src in range(DEVICES):
        mine, other = e_table[src, 0, CAP], e_table[src + 1 - 2 * (src % 2), 0, CAP]
        over = (mine > room).astype(jnp.int32) * (mine - room)
        free = (other < room).astype(jnp.int32) * (room - at_least(other, KEPT))
        wrong = wrong + (over > free).astype(jnp.int32)
    short[0] = (wrong > 0).astype(jnp.int32)

    pltpu.make_async_copy(t_in, t_in, t_sem).wait()
    get_pats = pltpu.make_async_copy(t_in, pats, local_sem.at[5])
    get_pats.start()
    get_pats.wait()

    for ref in lines:
        ref[blocks] = jnp.zeros((BS, BS), jnp.bfloat16)
        ref[half + blocks] = jnp.zeros((BS, BS), jnp.bfloat16)

    def tally(panel):
        number = jnp.int32(0)
        for b in range(blocks):
            number = number + pats[panel, b // TALL, b % TALL]
        tallies[panel] = number

    loop(0, COLS, tally)

    def locate(panel):
        kind = panel % 2
        start = kind * half
        beyond = (1 - kind) * half + at_least(tallies[panel + 1 - 2 * kind], KEPT)
        last_spot = (1 - kind) * half + blocks
        number = jnp.int32(0)
        for b in range(blocks):
            on = pats[panel, b // TALL, b % TALL]
            fits = (number < room).astype(jnp.int32)
            past = beyond + number - room
            past = past - (past > last_spot).astype(jnp.int32) * (past - last_spot)
            spot = fits * (start + number) + (1 - fits) * past
            place[panel, b] = on * spot + (1 - on) * blocks
            number = number + on

    loop(0, COLS, locate)

    def pass_on(d, ch):
        @pl.when(z >= d)
        def _():
            up(d - 1, ch).wait_recv()
            if d < LINE - 1:

                @pl.when(z < LINE - 1)
                def _():
                    up(d, ch).start()

            twin(d, ch).start()

        @pl.when(z + d < LINE)
        def _():
            down(d - 1, ch).wait_recv()
            if d < LINE - 1:

                @pl.when(z > 0)
                def _():
                    down(d, ch).start()

            twin(LINE - 1 + d, ch).start()

    def wait_twin(i):
        loop(0, PIECES, lambda ch: from_twin(i, ch).wait())

    def expand(ref, panel, ch):
        for i in range(STEP // BS):
            row = ch * (STEP // BS) + i
            for j in range(QB):
                block = ref[place[panel, j * TALL + row]]
                xg[panel, pl.ds(row * BS, BS), j * BS : (j + 1) * BS] = block

    def multiply(zp, ch):
        rows = pl.ds(ch * STEP, STEP)
        return jnp.dot(
            xg[2 * zp, rows, :], yg[zp, 0:HALF, :], preferred_element_type=jnp.float32
        ) + jnp.dot(
            xg[2 * zp + 1, rows, :], yg[zp, HALF : 2 * HALF, :], preferred_element_type=jnp.float32
        )

    def add(d):
        def panels(zp, i):
            wait_twin(i)

            def one(ch):
                expand(lines[i], 2 * zp, ch)
                expand(lines[i], 2 * zp + 1, ch)
                acc[pl.ds(ch * STEP, STEP), :] += multiply(zp, ch)

            loop(0, CHUNKS, one)

        @pl.when(z >= d)
        def _():
            panels(z - d, d)

        @pl.when(z + d < LINE)
        def _():
            panels(z + d, LINE - 1 + d)

    loop(0, 1, lambda ch: pass_on(1, ch))
    y_copy(row_x, 0, r, 0).wait_recv()
    y_copy(row_x, 0, row_y, 4).start()
    y_copy(row_y, 1, r, 1).wait_recv()
    y_copy(row_y, 1, row_x, 5).start()
    loop(1, PIECES, lambda ch: pass_on(1, ch))
    loop(0, 1, lambda ch: pass_on(2, ch))
    y_copy(row_x, 1, r, 2).wait_recv()
    y_copy(row_y, 0, r, 3).wait_recv()
    row_d = 3 - r
    y_copy(row_d, 0, r, 4).wait_recv()
    y_copy(row_d, 1, r, 5).wait_recv()
    wait_twin(0)

    def first(ch):
        expand(lines[0], 2 * z + 1 - core, ch)
        acc[pl.ds(ch * STEP, STEP), :] = multiply(z, ch)

    loop(0, CHUNKS, first)
    add(1)
    loop(1, PIECES, lambda ch: pass_on(2, ch))
    add(2)

    eye_f = eye.astype(jnp.float32)

    def finish(ch):
        for i in range(STEP // BS):
            block_row = ch * (STEP // BS) + i
            rows = pl.ds(ch * STEP + i * BS, BS)
            for j in range(QB):
                cols = slice(j * BS, (j + 1) * BS)
                keep = pat_p[j, block_row].astype(jnp.float32)
                xnew = 1.5 * xg[c, rows, cols].astype(jnp.float32) - 0.5 * (acc[rows, cols] * keep)
                sgn[rows, cols] = xnew.astype(jnp.bfloat16)
                on = jnp.where(r * 8 + block_row == c * QB + j, 0.5, 0.0).astype(jnp.float32)
                dens[block_row * QB + j] = (on * eye_f - 0.5 * xnew).astype(jnp.bfloat16)

    loop(0, PIECES, lambda ch: pass_on(3, ch))
    add(3)
    loop(0, CHUNKS, finish)

    put = pltpu.make_async_copy(sgn, sign_hbm, local_sem.at[4])
    put.start()

    def d_copy(o, src):
        return pltpu.make_async_remote_copy(
            src_ref=outbox.at[o],
            dst_ref=inbox.at[src],
            send_sem=dsend_sem,
            recv_sem=d_sem.at[src],
            device_id=(o // COLS, o % COLS),
            device_id_type=MESH,
        )

    inner = z * (LINE - 1 - z) // 2
    near = z + 1 - 2 * (z % 2)
    far = (z + 2) % LINE
    planes = (
        LINE - 1 - z,
        far + inner * (z - far),
        near + inner * (far - near),
        z + inner * (near - z),
    )
    for zz in planes:

        def send(j, zz=zz):
            o = (r + j // 2) % ROWS * COLS + zz * 2 + (core + j) % 2

            @pl.when(o != me)
            def _():
                for k in range(CAP):
                    outbox[o, k] = dens[table[o * CAP + k]]
                d_copy(o, me).start()

        loop(0, COLS, send)

    def force(s, block):
        parts[pl.ds(s, 1), :] = jnp.sum(block.astype(jnp.float32) * wbuf[s], axis=0, keepdims=True)

    for k in range(CAP):
        force(me * CAP + k, dens[table[me * CAP + k]])

    for zz in (1, 2, 0, 3):

        def take(j, zz=zz):
            src = (r + ROWS - j // 2) % ROWS * COLS + zz * 2 + (core + j) % 2

            @pl.when(src != me)
            def _():
                d_copy(src, src).wait_recv()
                for k in range(CAP):
                    force(src * CAP + k, inbox[src, k])

        loop(0, COLS, take)

    def sent(ch):
        twin(0, ch).wait_send()
        for d in range(LINE):

            @pl.when(z >= d)
            def _(d=d):
                if d:
                    twin(d, ch).wait_send()
                if d < LINE - 1:

                    @pl.when(z < LINE - 1)
                    def _():
                        up(d, ch).wait_send()

            @pl.when(z + d < LINE)
            def _(d=d):
                if d:
                    twin(LINE - 1 + d, ch).wait_send()
                if d < LINE - 1:

                    @pl.when(z > 0)
                    def _():
                        down(d, ch).wait_send()

    loop(0, PIECES, sent)
    if spill:
        hand_over.wait_send()
    for i in range(1, ROWS):
        row_copy(i).wait_send()
    y_copy(r, 0, row_x, 0).wait_send()
    y_copy(r, 1, row_y, 1).wait_send()
    y_copy(r, 1, row_x, 2).wait_send()
    y_copy(r, 0, row_y, 3).wait_send()
    y_copy(row_x, 0, row_y, 4).wait_send()
    y_copy(row_y, 1, row_x, 5).wait_send()
    out = t_in.at[pl.ds(0, COLS - 1)]
    pltpu.make_async_copy(out, out, tsend_sem).wait()
    out = e_out.at[pl.ds(0, DEVICES - 1)]
    pltpu.make_async_copy(out, out, esend_sem).wait()
    out = outbox.at[pl.ds(0, DEVICES - 1)]
    pltpu.make_async_copy(out, out, dsend_sem).wait()
    put.wait()


def fused(
    room,
    number,
    sign_iterate,
    sign_square,
    pattern_x,
    pattern_y,
    pattern_product,
    orbital_energy,
    pair_dest,
    pair_block,
    force_h,
    force_s,
):
    slots = DEVICES * CAP
    blocks = QB * TALL
    vmem = pl.BlockSpec(memory_space=pltpu.VMEM)
    smem = pl.BlockSpec(memory_space=pltpu.SMEM)
    hbm = pl.BlockSpec(memory_space=pl.ANY)
    bf16, f32, i32 = jnp.bfloat16, jnp.float32, jnp.int32
    dma = pltpu.SemaphoreType.DMA
    tile = sign_iterate.shape
    return pl.pallas_call(
        functools.partial(kernel, room),
        out_shape=(
            jax.ShapeDtypeStruct(tile, bf16),
            jax.ShapeDtypeStruct((slots, BS), f32),
            jax.ShapeDtypeStruct((1,), i32),
        ),
        in_specs=[smem] * 5 + [vmem] * 2 + [hbm] * 4,
        out_specs=(hbm, vmem, smem),
        scratch_shapes=[
            pltpu.VMEM((blocks + 1, BS, BS), bf16),
            [pltpu.VMEM((2 * blocks + 2, BS, BS), bf16)] * (2 * LINE - 1),
            pltpu.VMEM((max(blocks - room, 1), BS, BS), bf16),
            pltpu.VMEM((blocks - room + 1, BS, BS), bf16),
            pltpu.VMEM((COLS, *tile), bf16),
            pltpu.VMEM((ROWS, *tile), bf16),
            pltpu.VMEM(tile, f32),
            pltpu.VMEM((blocks + 1, BS, BS), bf16),
            pltpu.VMEM(tile, bf16),
            pltpu.VMEM((slots, BS, BS), bf16),
            pltpu.VMEM((slots, BS, BS), bf16),
            pltpu.VMEM((slots, BS, BS), f32),
            pltpu.VMEM((DEVICES, CAP, BS, BS), bf16),
            pltpu.VMEM((DEVICES, CAP, BS, BS), bf16),
            pltpu.VMEM((DEVICES, 1, BS), i32),
            pltpu.VMEM((DEVICES, 1, BS), i32),
            pltpu.SMEM((DEVICES, 1, BS), i32),
            pltpu.VMEM((ROWS, 2 * TALL, BS), f32),
            pltpu.VMEM((QB, BS), i32),
            pltpu.VMEM((COLS, QB, BS), i32),
            pltpu.SMEM((COLS, QB, BS), i32),
            pltpu.SMEM((blocks,), i32),
            pltpu.SMEM((blocks,), i32),
            pltpu.SMEM((COLS, blocks), i32),
            pltpu.SMEM((COLS,), i32),
            pltpu.SMEM((slots,), i32),
            dma((6,)),
            dma((LINE - 1, PIECES)),
            dma((LINE - 1, PIECES)),
            dma((2 * LINE - 1, PIECES)),
            dma((2 * LINE - 1, PIECES)),
            dma((2 * LINE - 1, PIECES)),
            dma((6,)),
            dma((ROWS, 2)),
            dma,
            dma,
            dma((DEVICES,)),
            dma,
            dma,
            dma,
            dma((2,)),
            dma((ROWS,)),
            dma((ROWS,)),
        ],
        compiler_params=pltpu.CompilerParams(
            collective_id=number, has_side_effects=True, vmem_limit_bytes=60 * 1024 * 1024
        ),
        cost_estimate=pl.CostEstimate(
            flops=2 * 1024 * 4096 * 512, bytes_accessed=8 * 1024 * 1024, transcendentals=0
        ),
        name=f"room_{room}",
    )(
        pattern_x.T,
        pattern_y.T,
        pattern_product.T,
        pair_dest[:, :, 0],
        pair_block,
        pattern_x.T,
        orbital_energy.reshape(-1, BS),
        sign_iterate.reshape(TALL, BS, tile[1]),
        sign_square,
        force_h,
        force_s,
    )


ROOM = 22


def adaptive(*arrays):
    sign_next, parts, short = fused(ROOM, 0, *arrays)
    sign_next, parts = lax.switch(
        short[0],
        (lambda: (sign_next, parts), lambda: tuple(fused(QB * TALL, 1, *arrays)[:2])),
    )
    return sign_next, jnp.sum(parts, axis=1)


def solution(mesh):
    in_specs = (
        P("row", "col"),
        P("row", "col"),
        P("row", "col"),
        P("row", "col"),
        P("row", "col"),
        P("row"),
        P(("row", "col"), None, None),
        P(("row", "col"), None),
        P(("row", "col"), None, None),
        P(("row", "col"), None, None),
    )
    out_specs = (P("row", "col"), P(("row", "col")))
    body = adaptive if (mesh.shape["row"], mesh.shape["col"]) == (ROWS, COLS) else shards
    return jax.shard_map(body, mesh=mesh, in_specs=in_specs, out_specs=out_specs, check_vma=False)
```

```python
import functools

import jax
import jax.numpy as jnp
from jax import lax
from jax.experimental import pallas as pl
from jax.experimental.pallas import tpu as pltpu
from jax.sharding import PartitionSpec as P

BS = 128
QB = 4
CAP = 2
MESH = pl.DeviceIdType.MESH


def masked_tile(tile, pattern):
    rows, cols = tile.shape
    shaped = tile.reshape(rows // BS, BS, cols // BS, BS) * pattern[:, None, :, None].astype(
        tile.dtype
    )
    return shaped.reshape(rows, cols)


def tile_blocks(tile):
    rows, cols = tile.shape
    shaped = tile.reshape(rows // BS, BS, cols // BS, BS).transpose(0, 2, 1, 3)
    return shaped.reshape(rows // BS * (cols // BS), BS * BS)


def rank_within(dest):
    entries = dest.shape[-1]
    order = jnp.arange(entries, dtype=jnp.int32)
    same = (dest[..., :, None] == dest[..., None, :]) & (order[None, :] < order[:, None])
    return jnp.sum(same.astype(jnp.int32), axis=-1)


def shards(
    sign_iterate,
    sign_square,
    pattern_x,
    pattern_y,
    pattern_product,
    orbital_energy,
    pair_dest,
    pair_block,
    force_h,
    force_s,
):
    rows_x, cols_x = sign_iterate.shape
    xmask = masked_tile(sign_iterate, pattern_x)
    ymask = masked_tile(sign_square, pattern_y)
    y_whole = lax.all_gather(ymask, "row", axis=0, tiled=True)
    product = jnp.dot(
        lax.all_gather(xmask, "col", axis=1, tiled=True),
        y_whole,
        preferred_element_type=jnp.float32,
    )
    product = masked_tile(product, pattern_product)
    xnew = 1.5 * xmask.astype(jnp.float32) - 0.5 * product
    sign_next = xnew.astype(jnp.bfloat16)
    global_rows = lax.axis_index("row") * rows_x + jnp.arange(rows_x, dtype=jnp.int32)
    global_cols = lax.axis_index("col") * cols_x + jnp.arange(cols_x, dtype=jnp.int32)
    identity = (global_rows[:, None] == global_cols[None, :]).astype(jnp.float32)
    density = (0.5 * identity - 0.5 * xnew).astype(jnp.bfloat16)
    dens_blocks = tile_blocks(density)
    n_rows = lax.axis_size("row")
    n_cols = lax.axis_size("col")
    devices = n_rows * n_cols
    slots = devices * CAP
    local_rows = rows_x // BS
    dest = pair_dest[0, :, 0]
    wanted = pair_block[0]
    rank = rank_within(dest)
    slot = dest * CAP + rank
    pick_slot = (jnp.arange(slots, dtype=jnp.int32)[:, None] == slot[None, :]).astype(jnp.bfloat16)
    pick_block = (
        wanted[:, None] == jnp.arange(dens_blocks.shape[0], dtype=jnp.int32)[None, :]
    ).astype(jnp.bfloat16)
    routing_table = jnp.dot(pick_slot, pick_block, preferred_element_type=jnp.float32).astype(
        jnp.bfloat16
    )
    send_dens = jnp.dot(routing_table, dens_blocks, preferred_element_type=jnp.float32).astype(
        jnp.bfloat16
    )
    pick_row = ((wanted // QB)[:, None] == jnp.arange(local_rows, dtype=jnp.int32)[None, :]).astype(
        jnp.bfloat16
    )
    slot_rows = jnp.dot(pick_slot, pick_row, preferred_element_type=jnp.float32).astype(
        jnp.bfloat16
    )
    send_energy = jnp.dot(
        slot_rows, orbital_energy.reshape(local_rows, BS), preferred_element_type=jnp.float32
    ).astype(jnp.bfloat16)
    payload = jnp.concatenate([send_dens.reshape(slots, BS, BS), send_energy[:, None, :]], axis=1)
    height = BS + 1
    received = lax.all_to_all(
        payload.reshape(devices, CAP, height * BS),
        ("row", "col"),
        split_axis=0,
        concat_axis=0,
        tiled=True,
    )
    received = received.reshape(slots, height, BS)
    recv_dens = received[:, :BS, :]
    energies = received[:, BS, :].astype(jnp.float32)
    h_term = jnp.einsum("sab,sab->s", recv_dens, force_h, preferred_element_type=jnp.float32)
    s_rows = jnp.einsum("sab,sab->sa", recv_dens, force_s, preferred_element_type=jnp.float32)
    forces = h_term - jnp.sum(energies * s_rows, axis=1)
    return (sign_next, forces)


ROWS = 4
COLS = 8
DEVICES = ROWS * COLS
LINE = 4
CHUNKS = 4
TALL = 8
STEP = 256
PIECES = 2
KEPT = 16
HALF = 512


def kernel(
    room,
    pat_x,
    pat_y,
    pat_p,
    dest,
    wanted,
    pat_tile,
    energy,
    x_hbm,
    y_hbm,
    h_hbm,
    s_hbm,
    sign_hbm,
    parts,
    short,
    xraw,
    lines,
    spill_out,
    spill_in,
    xg,
    yg,
    acc,
    dens,
    sgn,
    hbuf,
    sbuf,
    wbuf,
    outbox,
    inbox,
    e_out,
    e_in,
    e_table,
    e_rows,
    t_out,
    t_in,
    pats,
    ahead,
    listed,
    place,
    tallies,
    table,
    local_sem,
    up_sem,
    down_sem,
    twin_sem,
    x_sem,
    tx_sem,
    ysend_sem,
    y_sem,
    e_sem,
    esend_sem,
    d_sem,
    dsend_sem,
    t_sem,
    tsend_sem,
    spill_sem,
    rows_sem,
    rsend_sem,
):
    blocks = QB * TALL
    piece = room // PIECES
    spill = blocks - room
    r = lax.axis_index("row")
    c = lax.axis_index("col")
    me = r * COLS + c
    z = c // 2
    core = c % 2
    row_x = r + 1 - 2 * (r % 2)
    row_y = (r + 2) % 4

    barrier = pltpu.get_barrier_semaphore()

    def greet(i, carry):
        other = (me + i) % DEVICES
        pl.semaphore_signal(
            barrier, inc=1, device_id=(other // COLS, other % COLS), device_id_type=MESH
        )
        return carry

    lax.fori_loop(1, DEVICES, greet, 0)

    for j in range(QB):
        pltpu.make_async_copy(
            x_hbm.at[:, :, j * BS : (j + 1) * BS],
            xraw.at[pl.ds(j * TALL, TALL)],
            local_sem.at[0],
        ).start()
    whole = xraw.at[pl.ds(0, blocks)]
    get_x = pltpu.make_async_copy(whole, whole, local_sem.at[0])
    get_y = pltpu.make_async_copy(y_hbm, yg.at[r], local_sem.at[1])
    get_h = pltpu.make_async_copy(h_hbm, hbuf, local_sem.at[2])
    get_s = pltpu.make_async_copy(s_hbm, sbuf, local_sem.at[3])
    get_y.start()
    get_h.start()
    get_s.start()

    def loop(lo, hi, body):
        def step(i, carry):
            body(i)
            return carry

        lax.fori_loop(lo, hi, step, 0)

    half = blocks + 1

    def x_copy(src, dst, ch, col, send_sem, recv_sem):
        rows = pl.ds(core * half + ch * piece, piece)
        return pltpu.make_async_remote_copy(
            src_ref=lines[src].at[rows],
            dst_ref=lines[dst].at[rows],
            send_sem=send_sem,
            recv_sem=recv_sem,
            device_id=(r, col),
            device_id_type=MESH,
        )

    def up(d, ch):
        return x_copy(d, d + 1, ch, c + 2, up_sem.at[d, ch], x_sem.at[d + 1, ch])

    def down(d, ch):
        to = d + LINE
        src = to - 1 if d else 0
        return x_copy(src, to, ch, c - 2, down_sem.at[d, ch], x_sem.at[to, ch])

    twin_col = c + 1 - 2 * core

    def twin(i, ch):
        return x_copy(i, i, ch, twin_col, twin_sem.at[i, ch], tx_sem.at[i, ch])

    def from_twin(i, ch):
        rows = pl.ds((1 - core) * half + ch * piece, piece)
        return pltpu.make_async_copy(lines[i].at[rows], lines[i].at[rows], tx_sem.at[i, ch])

    def y_copy(owner, half, to, number):
        block = yg.at[owner, pl.ds(half * HALF, HALF)]
        return pltpu.make_async_remote_copy(
            src_ref=block,
            dst_ref=block,
            send_sem=ysend_sem.at[number],
            recv_sem=y_sem.at[owner, half],
            device_id=(to, c),
            device_id_type=MESH,
        )

    t_out[...] = jnp.zeros_like(t_out)
    t_out[0:QB, 0:TALL] = pat_tile[...]
    number = jnp.int32(0)
    for b in range(blocks):
        number = number + pat_x[b // TALL, b % TALL]
        ahead[b] = number
    count = number

    def seek(t):
        found = jnp.int32(0)
        for b in range(blocks):
            found = found + (ahead[b] <= t).astype(jnp.int32)
        listed[t] = found

    loop(0, blocks, seek)
    xraw[blocks] = jnp.zeros((BS, BS), jnp.bfloat16)

    def at_least(n, low):
        return low + (n > low).astype(jnp.int32) * (n - low)

    get_x.wait()

    early = KEPT if spill else room

    def compact(t):
        lines[0][core * half + t] = xraw[listed[t]]

    loop(0, early, compact)
    for t in range(spill):
        spill_out[t] = xraw[listed[room + t]]
    if spill:
        spill_in[spill] = jnp.zeros((BS, BS), jnp.bfloat16)
    pl.semaphore_wait(barrier, DEVICES - 1)

    def t_copy(col):
        return pltpu.make_async_remote_copy(
            src_ref=t_out,
            dst_ref=t_in.at[c],
            send_sem=tsend_sem,
            recv_sem=t_sem,
            device_id=(r, col),
            device_id_type=MESH,
        )

    loop(1, COLS, lambda i: t_copy((c + i) % COLS).start())
    pltpu.make_async_copy(t_out, t_in.at[c], t_sem).start()

    def send_x(ch):
        @pl.when(z < LINE - 1)
        def _():
            up(0, ch).start()

        @pl.when(z > 0)
        def _():
            down(0, ch).start()

        twin(0, ch).start()

    hand_over = None
    if spill:
        hand_over = pltpu.make_async_remote_copy(
            src_ref=spill_out,
            dst_ref=spill_in.at[pl.ds(0, spill)],
            send_sem=spill_sem.at[0],
            recv_sem=spill_sem.at[1],
            device_id=(r, twin_col),
            device_id_type=MESH,
        )
        hand_over.start()
    send_x(0)
    if spill:
        hand_over.wait_recv()
        used = at_least(count, KEPT)

        def fill(t):
            own = (t < count).astype(jnp.int32)
            extra = spill_in[own * spill + (1 - own) * (t - used) * (t >= used).astype(jnp.int32)]
            lines[0][core * half + t] = xraw[listed[t]] + extra

        loop(early, room, fill)
    loop(1, PIECES, send_x)
    get_y.wait()

    def mask_y(i):
        rows = pl.ds(i * BS, BS)
        for j in range(QB):
            cols = slice(j * BS, (j + 1) * BS)
            keep = pat_y[j, i].astype(jnp.float32)
            yg[r, rows, cols] = (yg[r, rows, cols].astype(jnp.float32) * keep).astype(jnp.bfloat16)

    loop(0, TALL, mask_y)
    y_copy(r, 0, row_x, 0).start()
    y_copy(r, 1, row_y, 1).start()
    y_copy(r, 1, row_x, 2).start()
    y_copy(r, 0, row_y, 3).start()

    def mask_x(i):
        rows = pl.ds(i * BS, BS)
        for j in range(QB):
            keep = pat_x[j, i].astype(jnp.float32)
            block = xraw[j * TALL + i].astype(jnp.float32) * keep
            xg[c, rows, j * BS : (j + 1) * BS] = block.astype(jnp.bfloat16)

    loop(0, TALL, mask_x)

    def find(o):
        seen = jnp.int32(0)
        slots = [jnp.int32(blocks)] * CAP
        for p in range(dest.shape[1]):
            hit = (dest[0, p] == o).astype(jnp.int32)
            for k in range(CAP):
                first_seen = hit * (seen == k).astype(jnp.int32)
                slots[k] = slots[k] + first_seen * (wanted[0, p] - blocks)
            seen = seen + hit
        for k in range(CAP):
            table[o * CAP + k] = slots[k]

    loop(0, DEVICES, find)
    lanes = lax.broadcasted_iota(jnp.int32, (1, BS), 1)

    def pack(o):
        line = jnp.full((1, BS), count)
        for k in range(CAP):
            line = jnp.where(lanes == k, table[o * CAP + k], line)
        e_out[o] = line

    loop(0, DEVICES, pack)

    def e_copy(o):
        return pltpu.make_async_remote_copy(
            src_ref=e_out.at[o],
            dst_ref=e_in.at[me],
            send_sem=esend_sem,
            recv_sem=e_sem,
            device_id=(o // COLS, o % COLS),
            device_id_type=MESH,
        )

    loop(1, DEVICES, lambda i: e_copy((me + i) % DEVICES).start())
    pltpu.make_async_copy(e_out.at[me], e_in.at[me], e_sem).start()

    for i in range(ROWS):
        e_rows[i, TALL : 2 * TALL, :] = jnp.zeros((TALL, BS), jnp.float32)
    own_rows = e_rows.at[r, pl.ds(0, TALL)]
    own_rows[...] = energy[...].astype(jnp.float32)

    def row_copy(i):
        return pltpu.make_async_remote_copy(
            src_ref=own_rows,
            dst_ref=own_rows,
            send_sem=rsend_sem.at[i],
            recv_sem=rows_sem.at[r],
            device_id=((r + i) % ROWS, c),
            device_id_type=MESH,
        )

    def row_arrival(i):
        other = (r + i) % ROWS
        ref = e_rows.at[other, pl.ds(0, TALL)]
        return pltpu.make_async_copy(ref, ref, rows_sem.at[other])

    for i in range(1, ROWS):
        row_copy(i).start()

    dens[QB * 8] = jnp.zeros((BS, BS), jnp.bfloat16)
    get_h.wait()
    get_s.wait()
    pltpu.make_async_copy(e_in, e_in, e_sem).wait()
    get_table = pltpu.make_async_copy(e_in, e_table, local_sem.at[5])
    get_table.start()
    get_table.wait()
    for i in range(1, ROWS):
        row_arrival(i).wait()

    eye = lax.broadcasted_iota(jnp.int32, (BS, BS), 0) == lax.broadcasted_iota(
        jnp.int32, (BS, BS), 1
    )

    def weigh(src, carry):
        for k in range(CAP):
            line = e_rows[src // COLS, pl.ds(e_table[src, 0, k] // QB, 1), :]
            line = jnp.broadcast_to(line, (BS, BS))
            col = jnp.sum(jnp.where(eye, line, 0.0), axis=1, keepdims=True)
            s = src * CAP + k
            wbuf[s] = hbuf[s].astype(jnp.float32) - col * sbuf[s].astype(jnp.float32)
        return carry

    lax.fori_loop(0, DEVICES, weigh, 0)

    wrong = jnp.int32(0)
    for src in range(DEVICES):
        mine, other = e_table[src, 0, CAP], e_table[src + 1 - 2 * (src % 2), 0, CAP]
        over = (mine > room).astype(jnp.int32) * (mine - room)
        free = (other < room).astype(jnp.int32) * (room - at_least(other, KEPT))
        wrong = wrong + (over > free).astype(jnp.int32)
    short[0] = (wrong > 0).astype(jnp.int32)

    pltpu.make_async_copy(t_in, t_in, t_sem).wait()
    get_pats = pltpu.make_async_copy(t_in, pats, local_sem.at[5])
    get_pats.start()
    get_pats.wait()

    for ref in lines:
        ref[blocks] = jnp.zeros((BS, BS), jnp.bfloat16)
        ref[half + blocks] = jnp.zeros((BS, BS), jnp.bfloat16)

    def tally(panel):
        number = jnp.int32(0)
        for b in range(blocks):
            number = number + pats[panel, b // TALL, b % TALL]
        tallies[panel] = number

    loop(0, COLS, tally)

    def locate(panel):
        kind = panel % 2
        start = kind * half
        beyond = (1 - kind) * half + at_least(tallies[panel + 1 - 2 * kind], KEPT)
        last_spot = (1 - kind) * half + blocks
        number = jnp.int32(0)
        for b in range(blocks):
            on = pats[panel, b // TALL, b % TALL]
            fits = (number < room).astype(jnp.int32)
            past = beyond + number - room
            past = past - (past > last_spot).astype(jnp.int32) * (past - last_spot)
            spot = fits * (start + number) + (1 - fits) * past
            place[panel, b] = on * spot + (1 - on) * blocks
            number = number + on

    loop(0, COLS, locate)

    def pass_on(d, ch):
        @pl.when(z >= d)
        def _():
            up(d - 1, ch).wait_recv()
            if d < LINE - 1:

                @pl.when(z < LINE - 1)
                def _():
                    up(d, ch).start()

            twin(d, ch).start()

        @pl.when(z + d < LINE)
        def _():
            down(d - 1, ch).wait_recv()
            if d < LINE - 1:

                @pl.when(z > 0)
                def _():
                    down(d, ch).start()

            twin(LINE - 1 + d, ch).start()

    def wait_twin(i):
        loop(0, PIECES, lambda ch: from_twin(i, ch).wait())

    def expand(ref, panel, ch):
        for i in range(STEP // BS):
            row = ch * (STEP // BS) + i
            for j in range(QB):
                block = ref[place[panel, j * TALL + row]]
                xg[panel, pl.ds(row * BS, BS), j * BS : (j + 1) * BS] = block

    def multiply(zp, ch):
        rows = pl.ds(ch * STEP, STEP)
        return jnp.dot(
            xg[2 * zp, rows, :], yg[zp, 0:HALF, :], preferred_element_type=jnp.float32
        ) + jnp.dot(
            xg[2 * zp + 1, rows, :], yg[zp, HALF : 2 * HALF, :], preferred_element_type=jnp.float32
        )

    def add(d):
        def panels(zp, i):
            wait_twin(i)

            def one(ch):
                expand(lines[i], 2 * zp, ch)
                expand(lines[i], 2 * zp + 1, ch)
                acc[pl.ds(ch * STEP, STEP), :] += multiply(zp, ch)

            loop(0, CHUNKS, one)

        @pl.when(z >= d)
        def _():
            panels(z - d, d)

        @pl.when(z + d < LINE)
        def _():
            panels(z + d, LINE - 1 + d)

    loop(0, 1, lambda ch: pass_on(1, ch))
    y_copy(row_x, 0, r, 0).wait_recv()
    y_copy(row_x, 0, row_y, 4).start()
    y_copy(row_y, 1, r, 1).wait_recv()
    y_copy(row_y, 1, row_x, 5).start()
    loop(1, PIECES, lambda ch: pass_on(1, ch))
    loop(0, 1, lambda ch: pass_on(2, ch))
    y_copy(row_x, 1, r, 2).wait_recv()
    y_copy(row_y, 0, r, 3).wait_recv()
    row_d = 3 - r
    y_copy(row_d, 0, r, 4).wait_recv()
    y_copy(row_d, 1, r, 5).wait_recv()
    wait_twin(0)

    def first(ch):
        expand(lines[0], 2 * z + 1 - core, ch)
        acc[pl.ds(ch * STEP, STEP), :] = multiply(z, ch)

    loop(0, CHUNKS, first)
    add(1)
    loop(1, PIECES, lambda ch: pass_on(2, ch))
    add(2)

    eye_f = eye.astype(jnp.float32)

    def finish(ch):
        for i in range(STEP // BS):
            block_row = ch * (STEP // BS) + i
            rows = pl.ds(ch * STEP + i * BS, BS)
            for j in range(QB):
                cols = slice(j * BS, (j + 1) * BS)
                keep = pat_p[j, block_row].astype(jnp.float32)
                xnew = 1.5 * xg[c, rows, cols].astype(jnp.float32) - 0.5 * (acc[rows, cols] * keep)
                sgn[rows, cols] = xnew.astype(jnp.bfloat16)
                on = jnp.where(r * 8 + block_row == c * QB + j, 0.5, 0.0).astype(jnp.float32)
                dens[block_row * QB + j] = (on * eye_f - 0.5 * xnew).astype(jnp.bfloat16)

    loop(0, PIECES, lambda ch: pass_on(3, ch))
    add(3)
    loop(0, CHUNKS, finish)

    put = pltpu.make_async_copy(sgn, sign_hbm, local_sem.at[4])
    put.start()

    def d_copy(o, src):
        return pltpu.make_async_remote_copy(
            src_ref=outbox.at[o],
            dst_ref=inbox.at[src],
            send_sem=dsend_sem,
            recv_sem=d_sem.at[src],
            device_id=(o // COLS, o % COLS),
            device_id_type=MESH,
        )

    def sent(ch):
        twin(0, ch).wait_send()
        for d in range(LINE):

            @pl.when(z >= d)
            def _(d=d):
                if d:
                    twin(d, ch).wait_send()
                if d < LINE - 1:

                    @pl.when(z < LINE - 1)
                    def _():
                        up(d, ch).wait_send()

            @pl.when(z + d < LINE)
            def _(d=d):
                if d:
                    twin(LINE - 1 + d, ch).wait_send()
                if d < LINE - 1:

                    @pl.when(z > 0)
                    def _():
                        down(d, ch).wait_send()

    inner = z * (LINE - 1 - z) // 2
    near = z + 1 - 2 * (z % 2)
    far = (z + 2) % LINE
    planes = (
        LINE - 1 - z,
        far + inner * (z - far),
        near + inner * (far - near),
        z + inner * (near - z),
    )
    for n, zz in enumerate(planes):
        if n == 2:
            loop(0, PIECES, sent)

        def send(j, zz=zz):
            o = (r + j // 2) % ROWS * COLS + zz * 2 + (core + j) % 2

            @pl.when(o != me)
            def _():
                for k in range(CAP):
                    outbox[o, k] = dens[table[o * CAP + k]]
                d_copy(o, me).start()

        loop(0, COLS, send)

    def force(s, block):
        parts[pl.ds(s, 1), :] = jnp.sum(block.astype(jnp.float32) * wbuf[s], axis=0, keepdims=True)

    for k in range(CAP):
        force(me * CAP + k, dens[table[me * CAP + k]])

    for zz in (1, 2, 0, 3):

        def take(j, zz=zz):
            src = (r + ROWS - j // 2) % ROWS * COLS + zz * 2 + (core + j) % 2

            @pl.when(src != me)
            def _():
                d_copy(src, src).wait_recv()
                for k in range(CAP):
                    force(src * CAP + k, inbox[src, k])

        loop(0, COLS, take)

    if spill:
        hand_over.wait_send()
    for i in range(1, ROWS):
        row_copy(i).wait_send()
    y_copy(r, 0, row_x, 0).wait_send()
    y_copy(r, 1, row_y, 1).wait_send()
    y_copy(r, 1, row_x, 2).wait_send()
    y_copy(r, 0, row_y, 3).wait_send()
    y_copy(row_x, 0, row_y, 4).wait_send()
    y_copy(row_y, 1, row_x, 5).wait_send()
    out = t_in.at[pl.ds(0, COLS - 1)]
    pltpu.make_async_copy(out, out, tsend_sem).wait()
    out = e_out.at[pl.ds(0, DEVICES - 1)]
    pltpu.make_async_copy(out, out, esend_sem).wait()
    out = outbox.at[pl.ds(0, DEVICES - 1)]
    pltpu.make_async_copy(out, out, dsend_sem).wait()
    put.wait()


def fused(
    room,
    number,
    sign_iterate,
    sign_square,
    pattern_x,
    pattern_y,
    pattern_product,
    orbital_energy,
    pair_dest,
    pair_block,
    force_h,
    force_s,
):
    slots = DEVICES * CAP
    blocks = QB * TALL
    vmem = pl.BlockSpec(memory_space=pltpu.VMEM)
    smem = pl.BlockSpec(memory_space=pltpu.SMEM)
    hbm = pl.BlockSpec(memory_space=pl.ANY)
    bf16, f32, i32 = jnp.bfloat16, jnp.float32, jnp.int32
    dma = pltpu.SemaphoreType.DMA
    tile = sign_iterate.shape
    return pl.pallas_call(
        functools.partial(kernel, room),
        out_shape=(
            jax.ShapeDtypeStruct(tile, bf16),
            jax.ShapeDtypeStruct((slots, BS), f32),
            jax.ShapeDtypeStruct((1,), i32),
        ),
        in_specs=[smem] * 5 + [vmem] * 2 + [hbm] * 4,
        out_specs=(hbm, vmem, smem),
        scratch_shapes=[
            pltpu.VMEM((blocks + 1, BS, BS), bf16),
            [pltpu.VMEM((2 * blocks + 2, BS, BS), bf16)] * (2 * LINE - 1),
            pltpu.VMEM((max(blocks - room, 1), BS, BS), bf16),
            pltpu.VMEM((blocks - room + 1, BS, BS), bf16),
            pltpu.VMEM((COLS, *tile), bf16),
            pltpu.VMEM((ROWS, *tile), bf16),
            pltpu.VMEM(tile, f32),
            pltpu.VMEM((blocks + 1, BS, BS), bf16),
            pltpu.VMEM(tile, bf16),
            pltpu.VMEM((slots, BS, BS), bf16),
            pltpu.VMEM((slots, BS, BS), bf16),
            pltpu.VMEM((slots, BS, BS), f32),
            pltpu.VMEM((DEVICES, CAP, BS, BS), bf16),
            pltpu.VMEM((DEVICES, CAP, BS, BS), bf16),
            pltpu.VMEM((DEVICES, 1, BS), i32),
            pltpu.VMEM((DEVICES, 1, BS), i32),
            pltpu.SMEM((DEVICES, 1, BS), i32),
            pltpu.VMEM((ROWS, 2 * TALL, BS), f32),
            pltpu.VMEM((QB, BS), i32),
            pltpu.VMEM((COLS, QB, BS), i32),
            pltpu.SMEM((COLS, QB, BS), i32),
            pltpu.SMEM((blocks,), i32),
            pltpu.SMEM((blocks,), i32),
            pltpu.SMEM((COLS, blocks), i32),
            pltpu.SMEM((COLS,), i32),
            pltpu.SMEM((slots,), i32),
            dma((6,)),
            dma((LINE - 1, PIECES)),
            dma((LINE - 1, PIECES)),
            dma((2 * LINE - 1, PIECES)),
            dma((2 * LINE - 1, PIECES)),
            dma((2 * LINE - 1, PIECES)),
            dma((6,)),
            dma((ROWS, 2)),
            dma,
            dma,
            dma((DEVICES,)),
            dma,
            dma,
            dma,
            dma((2,)),
            dma((ROWS,)),
            dma((ROWS,)),
        ],
        compiler_params=pltpu.CompilerParams(
            collective_id=number, has_side_effects=True, vmem_limit_bytes=60 * 1024 * 1024
        ),
        cost_estimate=pl.CostEstimate(
            flops=2 * 1024 * 4096 * 512, bytes_accessed=8 * 1024 * 1024, transcendentals=0
        ),
        name=f"room_{room}",
    )(
        pattern_x.T,
        pattern_y.T,
        pattern_product.T,
        pair_dest[:, :, 0],
        pair_block,
        pattern_x.T,
        orbital_energy.reshape(-1, BS),
        sign_iterate.reshape(TALL, BS, tile[1]),
        sign_square,
        force_h,
        force_s,
    )


ROOM = 22


def adaptive(*arrays):
    sign_next, parts, short = fused(ROOM, 0, *arrays)
    sign_next, parts = lax.switch(
        short[0],
        (lambda: (sign_next, parts), lambda: tuple(fused(QB * TALL, 1, *arrays)[:2])),
    )
    return sign_next, jnp.sum(parts, axis=1)


def solution(mesh):
    in_specs = (
        P("row", "col"),
        P("row", "col"),
        P("row", "col"),
        P("row", "col"),
        P("row", "col"),
        P("row"),
        P(("row", "col"), None, None),
        P(("row", "col"), None),
        P(("row", "col"), None, None),
        P(("row", "col"), None, None),
    )
    out_specs = (P("row", "col"), P(("row", "col")))
    body = adaptive if (mesh.shape["row"], mesh.shape["col"]) == (ROWS, COLS) else shards
    return jax.shard_map(body, mesh=mesh, in_specs=in_specs, out_specs=out_specs, check_vma=False)
```

```python
import functools

import jax
import jax.numpy as jnp
from jax import lax
from jax.experimental import pallas as pl
from jax.experimental.pallas import tpu as pltpu
from jax.sharding import PartitionSpec as P

BS = 128
QB = 4
CAP = 2
MESH = pl.DeviceIdType.MESH


def masked_tile(tile, pattern):
    rows, cols = tile.shape
    shaped = tile.reshape(rows // BS, BS, cols // BS, BS) * pattern[:, None, :, None].astype(
        tile.dtype
    )
    return shaped.reshape(rows, cols)


def tile_blocks(tile):
    rows, cols = tile.shape
    shaped = tile.reshape(rows // BS, BS, cols // BS, BS).transpose(0, 2, 1, 3)
    return shaped.reshape(rows // BS * (cols // BS), BS * BS)


def rank_within(dest):
    entries = dest.shape[-1]
    order = jnp.arange(entries, dtype=jnp.int32)
    same = (dest[..., :, None] == dest[..., None, :]) & (order[None, :] < order[:, None])
    return jnp.sum(same.astype(jnp.int32), axis=-1)


def shards(
    sign_iterate,
    sign_square,
    pattern_x,
    pattern_y,
    pattern_product,
    orbital_energy,
    pair_dest,
    pair_block,
    force_h,
    force_s,
):
    rows_x, cols_x = sign_iterate.shape
    xmask = masked_tile(sign_iterate, pattern_x)
    ymask = masked_tile(sign_square, pattern_y)
    y_whole = lax.all_gather(ymask, "row", axis=0, tiled=True)
    product = jnp.dot(
        lax.all_gather(xmask, "col", axis=1, tiled=True),
        y_whole,
        preferred_element_type=jnp.float32,
    )
    product = masked_tile(product, pattern_product)
    xnew = 1.5 * xmask.astype(jnp.float32) - 0.5 * product
    sign_next = xnew.astype(jnp.bfloat16)
    global_rows = lax.axis_index("row") * rows_x + jnp.arange(rows_x, dtype=jnp.int32)
    global_cols = lax.axis_index("col") * cols_x + jnp.arange(cols_x, dtype=jnp.int32)
    identity = (global_rows[:, None] == global_cols[None, :]).astype(jnp.float32)
    density = (0.5 * identity - 0.5 * xnew).astype(jnp.bfloat16)
    dens_blocks = tile_blocks(density)
    n_rows = lax.axis_size("row")
    n_cols = lax.axis_size("col")
    devices = n_rows * n_cols
    slots = devices * CAP
    local_rows = rows_x // BS
    dest = pair_dest[0, :, 0]
    wanted = pair_block[0]
    rank = rank_within(dest)
    slot = dest * CAP + rank
    pick_slot = (jnp.arange(slots, dtype=jnp.int32)[:, None] == slot[None, :]).astype(jnp.bfloat16)
    pick_block = (
        wanted[:, None] == jnp.arange(dens_blocks.shape[0], dtype=jnp.int32)[None, :]
    ).astype(jnp.bfloat16)
    routing_table = jnp.dot(pick_slot, pick_block, preferred_element_type=jnp.float32).astype(
        jnp.bfloat16
    )
    send_dens = jnp.dot(routing_table, dens_blocks, preferred_element_type=jnp.float32).astype(
        jnp.bfloat16
    )
    pick_row = ((wanted // QB)[:, None] == jnp.arange(local_rows, dtype=jnp.int32)[None, :]).astype(
        jnp.bfloat16
    )
    slot_rows = jnp.dot(pick_slot, pick_row, preferred_element_type=jnp.float32).astype(
        jnp.bfloat16
    )
    send_energy = jnp.dot(
        slot_rows, orbital_energy.reshape(local_rows, BS), preferred_element_type=jnp.float32
    ).astype(jnp.bfloat16)
    payload = jnp.concatenate([send_dens.reshape(slots, BS, BS), send_energy[:, None, :]], axis=1)
    height = BS + 1
    received = lax.all_to_all(
        payload.reshape(devices, CAP, height * BS),
        ("row", "col"),
        split_axis=0,
        concat_axis=0,
        tiled=True,
    )
    received = received.reshape(slots, height, BS)
    recv_dens = received[:, :BS, :]
    energies = received[:, BS, :].astype(jnp.float32)
    h_term = jnp.einsum("sab,sab->s", recv_dens, force_h, preferred_element_type=jnp.float32)
    s_rows = jnp.einsum("sab,sab->sa", recv_dens, force_s, preferred_element_type=jnp.float32)
    forces = h_term - jnp.sum(energies * s_rows, axis=1)
    return (sign_next, forces)


ROWS = 4
COLS = 8
DEVICES = ROWS * COLS
LINE = 4
CHUNKS = 4
TALL = 8
STEP = 256
PIECES = 2
KEPT = 16
HALF = 512


def kernel(
    room,
    pat_x,
    pat_y,
    pat_p,
    dest,
    wanted,
    pat_tile,
    energy,
    x_hbm,
    y_hbm,
    h_hbm,
    s_hbm,
    sign_hbm,
    parts,
    short,
    xraw,
    lines,
    spill_out,
    spill_in,
    xg,
    yg,
    acc,
    dens,
    sgn,
    hbuf,
    sbuf,
    wbuf,
    outbox,
    inbox,
    e_out,
    e_in,
    e_table,
    e_rows,
    t_out,
    t_in,
    pats,
    ahead,
    listed,
    place,
    tallies,
    table,
    local_sem,
    up_sem,
    down_sem,
    twin_sem,
    x_sem,
    tx_sem,
    ysend_sem,
    y_sem,
    e_sem,
    esend_sem,
    d_sem,
    dsend_sem,
    t_sem,
    tsend_sem,
    spill_sem,
    rows_sem,
    rsend_sem,
):
    blocks = QB * TALL
    piece = room // PIECES
    spill = blocks - room
    r = lax.axis_index("row")
    c = lax.axis_index("col")
    me = r * COLS + c
    z = c // 2
    core = c % 2
    row_x = r + 1 - 2 * (r % 2)
    row_y = (r + 2) % 4

    barrier = pltpu.get_barrier_semaphore()

    def greet(i, carry):
        other = (me + i) % DEVICES
        pl.semaphore_signal(
            barrier, inc=1, device_id=(other // COLS, other % COLS), device_id_type=MESH
        )
        return carry

    lax.fori_loop(1, DEVICES, greet, 0)

    for j in range(QB):
        pltpu.make_async_copy(
            x_hbm.at[:, :, j * BS : (j + 1) * BS],
            xraw.at[pl.ds(j * TALL, TALL)],
            local_sem.at[0],
        ).start()
    whole = xraw.at[pl.ds(0, blocks)]
    get_x = pltpu.make_async_copy(whole, whole, local_sem.at[0])
    get_y = pltpu.make_async_copy(y_hbm, yg.at[r], local_sem.at[1])
    get_h = pltpu.make_async_copy(h_hbm, hbuf, local_sem.at[2])
    get_s = pltpu.make_async_copy(s_hbm, sbuf, local_sem.at[3])
    get_y.start()
    get_h.start()
    get_s.start()

    def loop(lo, hi, body):
        def step(i, carry):
            body(i)
            return carry

        lax.fori_loop(lo, hi, step, 0)

    half = blocks + 1

    def x_copy(src, dst, ch, col, send_sem, recv_sem):
        rows = pl.ds(core * half + ch * piece, piece)
        return pltpu.make_async_remote_copy(
            src_ref=lines[src].at[rows],
            dst_ref=lines[dst].at[rows],
            send_sem=send_sem,
            recv_sem=recv_sem,
            device_id=(r, col),
            device_id_type=MESH,
        )

    def up(d, ch):
        return x_copy(d, d + 1, ch, c + 2, up_sem.at[d, ch], x_sem.at[d + 1, ch])

    def down(d, ch):
        to = d + LINE
        src = to - 1 if d else 0
        return x_copy(src, to, ch, c - 2, down_sem.at[d, ch], x_sem.at[to, ch])

    twin_col = c + 1 - 2 * core

    def twin(i, ch):
        return x_copy(i, i, ch, twin_col, twin_sem.at[i, ch], tx_sem.at[i, ch])

    def from_twin(i, ch):
        rows = pl.ds((1 - core) * half + ch * piece, piece)
        return pltpu.make_async_copy(lines[i].at[rows], lines[i].at[rows], tx_sem.at[i, ch])

    def y_copy(owner, half, to, number):
        block = yg.at[owner, pl.ds(half * HALF, HALF)]
        return pltpu.make_async_remote_copy(
            src_ref=block,
            dst_ref=block,
            send_sem=ysend_sem.at[number],
            recv_sem=y_sem.at[owner, half],
            device_id=(to, c),
            device_id_type=MESH,
        )

    t_out[...] = jnp.zeros_like(t_out)
    t_out[0:QB, 0:TALL] = pat_tile[...]
    number = jnp.int32(0)
    for b in range(blocks):
        number = number + pat_x[b // TALL, b % TALL]
        ahead[b] = number
    count = number

    def seek(t):
        found = jnp.int32(0)
        for b in range(blocks):
            found = found + (ahead[b] <= t).astype(jnp.int32)
        listed[t] = found

    loop(0, blocks, seek)
    xraw[blocks] = jnp.zeros((BS, BS), jnp.bfloat16)

    def at_least(n, low):
        return low + (n > low).astype(jnp.int32) * (n - low)

    get_x.wait()

    early = KEPT if spill else room

    def compact(t):
        lines[0][core * half + t] = xraw[listed[t]]

    loop(0, early, compact)
    for t in range(spill):
        spill_out[t] = xraw[listed[room + t]]
    if spill:
        spill_in[spill] = jnp.zeros((BS, BS), jnp.bfloat16)
    pl.semaphore_wait(barrier, DEVICES - 1)

    def t_copy(col):
        return pltpu.make_async_remote_copy(
            src_ref=t_out,
            dst_ref=t_in.at[c],
            send_sem=tsend_sem,
            recv_sem=t_sem,
            device_id=(r, col),
            device_id_type=MESH,
        )

    loop(1, COLS, lambda i: t_copy((c + i) % COLS).start())
    pltpu.make_async_copy(t_out, t_in.at[c], t_sem).start()

    def send_x(ch):
        @pl.when(z < LINE - 1)
        def _():
            up(0, ch).start()

        @pl.when(z > 0)
        def _():
            down(0, ch).start()

        twin(0, ch).start()

    hand_over = None
    if spill:
        hand_over = pltpu.make_async_remote_copy(
            src_ref=spill_out,
            dst_ref=spill_in.at[pl.ds(0, spill)],
            send_sem=spill_sem.at[0],
            recv_sem=spill_sem.at[1],
            device_id=(r, twin_col),
            device_id_type=MESH,
        )
        hand_over.start()
    send_x(0)
    if spill:
        hand_over.wait_recv()
        used = at_least(count, KEPT)

        def fill(t):
            own = (t < count).astype(jnp.int32)
            extra = spill_in[own * spill + (1 - own) * (t - used) * (t >= used).astype(jnp.int32)]
            lines[0][core * half + t] = xraw[listed[t]] + extra

        loop(early, room, fill)
    loop(1, PIECES, send_x)
    get_y.wait()

    def mask_y(i):
        rows = pl.ds(i * BS, BS)
        for j in range(QB):
            cols = slice(j * BS, (j + 1) * BS)
            keep = pat_y[j, i].astype(jnp.float32)
            yg[r, rows, cols] = (yg[r, rows, cols].astype(jnp.float32) * keep).astype(jnp.bfloat16)

    loop(0, TALL, mask_y)
    y_copy(r, 0, row_x, 0).start()
    y_copy(r, 1, row_y, 1).start()
    y_copy(r, 1, row_x, 2).start()
    y_copy(r, 0, row_y, 3).start()

    def mask_x(i):
        rows = pl.ds(i * BS, BS)
        for j in range(QB):
            keep = pat_x[j, i].astype(jnp.float32)
            block = xraw[j * TALL + i].astype(jnp.float32) * keep
            xg[c, rows, j * BS : (j + 1) * BS] = block.astype(jnp.bfloat16)

    loop(0, TALL, mask_x)

    def find(o):
        seen = jnp.int32(0)
        slots = [jnp.int32(blocks)] * CAP
        for p in range(dest.shape[1]):
            hit = (dest[0, p] == o).astype(jnp.int32)
            for k in range(CAP):
                first_seen = hit * (seen == k).astype(jnp.int32)
                slots[k] = slots[k] + first_seen * (wanted[0, p] - blocks)
            seen = seen + hit
        for k in range(CAP):
            table[o * CAP + k] = slots[k]

    loop(0, DEVICES, find)
    lanes = lax.broadcasted_iota(jnp.int32, (1, BS), 1)

    def pack(o):
        line = jnp.full((1, BS), count)
        for k in range(CAP):
            line = jnp.where(lanes == k, table[o * CAP + k], line)
        e_out[o] = line

    loop(0, DEVICES, pack)

    def e_copy(o):
        return pltpu.make_async_remote_copy(
            src_ref=e_out.at[o],
            dst_ref=e_in.at[me],
            send_sem=esend_sem,
            recv_sem=e_sem,
            device_id=(o // COLS, o % COLS),
            device_id_type=MESH,
        )

    loop(1, DEVICES, lambda i: e_copy((me + i) % DEVICES).start())
    pltpu.make_async_copy(e_out.at[me], e_in.at[me], e_sem).start()

    for i in range(ROWS):
        e_rows[i, TALL : 2 * TALL, :] = jnp.zeros((TALL, BS), jnp.float32)
    own_rows = e_rows.at[r, pl.ds(0, TALL)]
    own_rows[...] = energy[...].astype(jnp.float32)

    def row_copy(i):
        return pltpu.make_async_remote_copy(
            src_ref=own_rows,
            dst_ref=own_rows,
            send_sem=rsend_sem.at[i],
            recv_sem=rows_sem.at[r],
            device_id=((r + i) % ROWS, c),
            device_id_type=MESH,
        )

    def row_arrival(i):
        other = (r + i) % ROWS
        ref = e_rows.at[other, pl.ds(0, TALL)]
        return pltpu.make_async_copy(ref, ref, rows_sem.at[other])

    for i in range(1, ROWS):
        row_copy(i).start()

    def pass_on(d, ch):
        @pl.when(z >= d)
        def _():
            up(d - 1, ch).wait_recv()
            if d < LINE - 1:

                @pl.when(z < LINE - 1)
                def _():
                    up(d, ch).start()

            twin(d, ch).start()

        @pl.when(z + d < LINE)
        def _():
            down(d - 1, ch).wait_recv()
            if d < LINE - 1:

                @pl.when(z > 0)
                def _():
                    down(d, ch).start()

            twin(LINE - 1 + d, ch).start()

    def wait_twin(i):
        loop(0, PIECES, lambda ch: from_twin(i, ch).wait())

    def expand(ref, panel, ch):
        for i in range(STEP // BS):
            row = ch * (STEP // BS) + i
            for j in range(QB):
                block = ref[place[panel, j * TALL + row]]
                xg[panel, pl.ds(row * BS, BS), j * BS : (j + 1) * BS] = block

    def multiply(zp, ch):
        rows = pl.ds(ch * STEP, STEP)
        return jnp.dot(
            xg[2 * zp, rows, :], yg[zp, 0:HALF, :], preferred_element_type=jnp.float32
        ) + jnp.dot(
            xg[2 * zp + 1, rows, :], yg[zp, HALF : 2 * HALF, :], preferred_element_type=jnp.float32
        )

    def add(d):
        def panels(zp, i):
            wait_twin(i)

            def one(ch):
                expand(lines[i], 2 * zp, ch)
                expand(lines[i], 2 * zp + 1, ch)
                acc[pl.ds(ch * STEP, STEP), :] += multiply(zp, ch)

            loop(0, CHUNKS, one)

        @pl.when(z >= d)
        def _():
            panels(z - d, d)

        @pl.when(z + d < LINE)
        def _():
            panels(z + d, LINE - 1 + d)

    loop(0, 1, lambda ch: pass_on(1, ch))

    pltpu.make_async_copy(t_in, t_in, t_sem).wait()
    get_pats = pltpu.make_async_copy(t_in, pats, local_sem.at[5])
    get_pats.start()
    get_pats.wait()

    for ref in lines:
        ref[blocks] = jnp.zeros((BS, BS), jnp.bfloat16)
        ref[half + blocks] = jnp.zeros((BS, BS), jnp.bfloat16)

    def tally(panel):
        number = jnp.int32(0)
        for b in range(blocks):
            number = number + pats[panel, b // TALL, b % TALL]
        tallies[panel] = number

    loop(0, COLS, tally)

    def locate(panel):
        kind = panel % 2
        start = kind * half
        beyond = (1 - kind) * half + at_least(tallies[panel + 1 - 2 * kind], KEPT)
        last_spot = (1 - kind) * half + blocks
        number = jnp.int32(0)
        for b in range(blocks):
            on = pats[panel, b // TALL, b % TALL]
            fits = (number < room).astype(jnp.int32)
            past = beyond + number - room
            past = past - (past > last_spot).astype(jnp.int32) * (past - last_spot)
            spot = fits * (start + number) + (1 - fits) * past
            place[panel, b] = on * spot + (1 - on) * blocks
            number = number + on

    loop(0, COLS, locate)

    loop(1, PIECES, lambda ch: pass_on(1, ch))

    dens[QB * 8] = jnp.zeros((BS, BS), jnp.bfloat16)
    get_h.wait()
    get_s.wait()
    pltpu.make_async_copy(e_in, e_in, e_sem).wait()
    get_table = pltpu.make_async_copy(e_in, e_table, local_sem.at[5])
    get_table.start()
    get_table.wait()
    for i in range(1, ROWS):
        row_arrival(i).wait()

    eye = lax.broadcasted_iota(jnp.int32, (BS, BS), 0) == lax.broadcasted_iota(
        jnp.int32, (BS, BS), 1
    )

    def weigh(src, carry):
        for k in range(CAP):
            line = e_rows[src // COLS, pl.ds(e_table[src, 0, k] // QB, 1), :]
            line = jnp.broadcast_to(line, (BS, BS))
            col = jnp.sum(jnp.where(eye, line, 0.0), axis=1, keepdims=True)
            s = src * CAP + k
            wbuf[s] = hbuf[s].astype(jnp.float32) - col * sbuf[s].astype(jnp.float32)
        return carry

    lax.fori_loop(0, DEVICES, weigh, 0)

    wrong = jnp.int32(0)
    for src in range(DEVICES):
        mine, other = e_table[src, 0, CAP], e_table[src + 1 - 2 * (src % 2), 0, CAP]
        over = (mine > room).astype(jnp.int32) * (mine - room)
        free = (other < room).astype(jnp.int32) * (room - at_least(other, KEPT))
        wrong = wrong + (over > free).astype(jnp.int32)
    short[0] = (wrong > 0).astype(jnp.int32)

    y_copy(row_x, 0, r, 0).wait_recv()
    y_copy(row_x, 0, row_y, 4).start()
    y_copy(row_y, 1, r, 1).wait_recv()
    y_copy(row_y, 1, row_x, 5).start()
    loop(0, PIECES, lambda ch: pass_on(2, ch))
    y_copy(row_x, 1, r, 2).wait_recv()
    y_copy(row_y, 0, r, 3).wait_recv()
    row_d = 3 - r
    y_copy(row_d, 0, r, 4).wait_recv()
    y_copy(row_d, 1, r, 5).wait_recv()
    wait_twin(0)

    def first(ch):
        expand(lines[0], 2 * z + 1 - core, ch)
        acc[pl.ds(ch * STEP, STEP), :] = multiply(z, ch)

    loop(0, CHUNKS, first)
    add(1)
    add(2)

    eye_f = eye.astype(jnp.float32)

    def finish(ch):
        for i in range(STEP // BS):
            block_row = ch * (STEP // BS) + i
            rows = pl.ds(ch * STEP + i * BS, BS)
            for j in range(QB):
                cols = slice(j * BS, (j + 1) * BS)
                keep = pat_p[j, block_row].astype(jnp.float32)
                xnew = 1.5 * xg[c, rows, cols].astype(jnp.float32) - 0.5 * (acc[rows, cols] * keep)
                sgn[rows, cols] = xnew.astype(jnp.bfloat16)
                on = jnp.where(r * 8 + block_row == c * QB + j, 0.5, 0.0).astype(jnp.float32)
                dens[block_row * QB + j] = (on * eye_f - 0.5 * xnew).astype(jnp.bfloat16)

    loop(0, PIECES, lambda ch: pass_on(3, ch))
    add(3)
    loop(0, CHUNKS, finish)

    put = pltpu.make_async_copy(sgn, sign_hbm, local_sem.at[4])
    put.start()

    def d_copy(o, src):
        return pltpu.make_async_remote_copy(
            src_ref=outbox.at[o],
            dst_ref=inbox.at[src],
            send_sem=dsend_sem,
            recv_sem=d_sem.at[src],
            device_id=(o // COLS, o % COLS),
            device_id_type=MESH,
        )

    def sent(ch):
        twin(0, ch).wait_send()
        for d in range(LINE):

            @pl.when(z >= d)
            def _(d=d):
                if d:
                    twin(d, ch).wait_send()
                if d < LINE - 1:

                    @pl.when(z < LINE - 1)
                    def _():
                        up(d, ch).wait_send()

            @pl.when(z + d < LINE)
            def _(d=d):
                if d:
                    twin(LINE - 1 + d, ch).wait_send()
                if d < LINE - 1:

                    @pl.when(z > 0)
                    def _():
                        down(d, ch).wait_send()

    inner = z * (LINE - 1 - z) // 2
    near = z + 1 - 2 * (z % 2)
    far = (z + 2) % LINE
    planes = (
        LINE - 1 - z,
        far + inner * (z - far),
        near + inner * (far - near),
        z + inner * (near - z),
    )
    for n, zz in enumerate(planes):
        if n == 2:
            loop(0, PIECES, sent)

        def send(j, zz=zz):
            o = (r + j // 2) % ROWS * COLS + zz * 2 + (core + j) % 2

            @pl.when(o != me)
            def _():
                for k in range(CAP):
                    outbox[o, k] = dens[table[o * CAP + k]]
                d_copy(o, me).start()

        loop(0, COLS, send)

    def force(s, block):
        parts[pl.ds(s, 1), :] = jnp.sum(block.astype(jnp.float32) * wbuf[s], axis=0, keepdims=True)

    for k in range(CAP):
        force(me * CAP + k, dens[table[me * CAP + k]])

    for zz in (1, 2, 0, 3):

        def take(j, zz=zz):
            src = (r + ROWS - j // 2) % ROWS * COLS + zz * 2 + (core + j) % 2

            @pl.when(src != me)
            def _():
                d_copy(src, src).wait_recv()
                for k in range(CAP):
                    force(src * CAP + k, inbox[src, k])

        loop(0, COLS, take)

    if spill:
        hand_over.wait_send()
    for i in range(1, ROWS):
        row_copy(i).wait_send()
    y_copy(r, 0, row_x, 0).wait_send()
    y_copy(r, 1, row_y, 1).wait_send()
    y_copy(r, 1, row_x, 2).wait_send()
    y_copy(r, 0, row_y, 3).wait_send()
    y_copy(row_x, 0, row_y, 4).wait_send()
    y_copy(row_y, 1, row_x, 5).wait_send()
    out = t_in.at[pl.ds(0, COLS - 1)]
    pltpu.make_async_copy(out, out, tsend_sem).wait()
    out = e_out.at[pl.ds(0, DEVICES - 1)]
    pltpu.make_async_copy(out, out, esend_sem).wait()
    out = outbox.at[pl.ds(0, DEVICES - 1)]
    pltpu.make_async_copy(out, out, dsend_sem).wait()
    put.wait()


def fused(
    room,
    number,
    sign_iterate,
    sign_square,
    pattern_x,
    pattern_y,
    pattern_product,
    orbital_energy,
    pair_dest,
    pair_block,
    force_h,
    force_s,
):
    slots = DEVICES * CAP
    blocks = QB * TALL
    vmem = pl.BlockSpec(memory_space=pltpu.VMEM)
    smem = pl.BlockSpec(memory_space=pltpu.SMEM)
    hbm = pl.BlockSpec(memory_space=pl.ANY)
    bf16, f32, i32 = jnp.bfloat16, jnp.float32, jnp.int32
    dma = pltpu.SemaphoreType.DMA
    tile = sign_iterate.shape
    return pl.pallas_call(
        functools.partial(kernel, room),
        out_shape=(
            jax.ShapeDtypeStruct(tile, bf16),
            jax.ShapeDtypeStruct((slots, BS), f32),
            jax.ShapeDtypeStruct((1,), i32),
        ),
        in_specs=[smem] * 5 + [vmem] * 2 + [hbm] * 4,
        out_specs=(hbm, vmem, smem),
        scratch_shapes=[
            pltpu.VMEM((blocks + 1, BS, BS), bf16),
            [pltpu.VMEM((2 * blocks + 2, BS, BS), bf16)] * (2 * LINE - 1),
            pltpu.VMEM((max(blocks - room, 1), BS, BS), bf16),
            pltpu.VMEM((blocks - room + 1, BS, BS), bf16),
            pltpu.VMEM((COLS, *tile), bf16),
            pltpu.VMEM((ROWS, *tile), bf16),
            pltpu.VMEM(tile, f32),
            pltpu.VMEM((blocks + 1, BS, BS), bf16),
            pltpu.VMEM(tile, bf16),
            pltpu.VMEM((slots, BS, BS), bf16),
            pltpu.VMEM((slots, BS, BS), bf16),
            pltpu.VMEM((slots, BS, BS), f32),
            pltpu.VMEM((DEVICES, CAP, BS, BS), bf16),
            pltpu.VMEM((DEVICES, CAP, BS, BS), bf16),
            pltpu.VMEM((DEVICES, 1, BS), i32),
            pltpu.VMEM((DEVICES, 1, BS), i32),
            pltpu.SMEM((DEVICES, 1, BS), i32),
            pltpu.VMEM((ROWS, 2 * TALL, BS), f32),
            pltpu.VMEM((QB, BS), i32),
            pltpu.VMEM((COLS, QB, BS), i32),
            pltpu.SMEM((COLS, QB, BS), i32),
            pltpu.SMEM((blocks,), i32),
            pltpu.SMEM((blocks,), i32),
            pltpu.SMEM((COLS, blocks), i32),
            pltpu.SMEM((COLS,), i32),
            pltpu.SMEM((slots,), i32),
            dma((6,)),
            dma((LINE - 1, PIECES)),
            dma((LINE - 1, PIECES)),
            dma((2 * LINE - 1, PIECES)),
            dma((2 * LINE - 1, PIECES)),
            dma((2 * LINE - 1, PIECES)),
            dma((6,)),
            dma((ROWS, 2)),
            dma,
            dma,
            dma((DEVICES,)),
            dma,
            dma,
            dma,
            dma((2,)),
            dma((ROWS,)),
            dma((ROWS,)),
        ],
        compiler_params=pltpu.CompilerParams(
            collective_id=number, has_side_effects=True, vmem_limit_bytes=60 * 1024 * 1024
        ),
        cost_estimate=pl.CostEstimate(
            flops=2 * 1024 * 4096 * 512, bytes_accessed=8 * 1024 * 1024, transcendentals=0
        ),
        name=f"room_{room}",
    )(
        pattern_x.T,
        pattern_y.T,
        pattern_product.T,
        pair_dest[:, :, 0],
        pair_block,
        pattern_x.T,
        orbital_energy.reshape(-1, BS),
        sign_iterate.reshape(TALL, BS, tile[1]),
        sign_square,
        force_h,
        force_s,
    )


ROOM = 22


def adaptive(*arrays):
    sign_next, parts, short = fused(ROOM, 0, *arrays)
    sign_next, parts = lax.switch(
        short[0],
        (lambda: (sign_next, parts), lambda: tuple(fused(QB * TALL, 1, *arrays)[:2])),
    )
    return sign_next, jnp.sum(parts, axis=1)


def solution(mesh):
    in_specs = (
        P("row", "col"),
        P("row", "col"),
        P("row", "col"),
        P("row", "col"),
        P("row", "col"),
        P("row"),
        P(("row", "col"), None, None),
        P(("row", "col"), None),
        P(("row", "col"), None, None),
        P(("row", "col"), None, None),
    )
    out_specs = (P("row", "col"), P(("row", "col")))
    body = adaptive if (mesh.shape["row"], mesh.shape["col"]) == (ROWS, COLS) else shards
    return jax.shard_map(body, mesh=mesh, in_specs=in_specs, out_specs=out_specs, check_vma=False)
```

```python
import functools

import jax
import jax.numpy as jnp
from jax import lax
from jax.experimental import pallas as pl
from jax.experimental.pallas import tpu as pltpu
from jax.sharding import PartitionSpec as P

BS = 128
QB = 4
CAP = 2
MESH = pl.DeviceIdType.MESH


def masked_tile(tile, pattern):
    rows, cols = tile.shape
    shaped = tile.reshape(rows // BS, BS, cols // BS, BS) * pattern[:, None, :, None].astype(
        tile.dtype
    )
    return shaped.reshape(rows, cols)


def tile_blocks(tile):
    rows, cols = tile.shape
    shaped = tile.reshape(rows // BS, BS, cols // BS, BS).transpose(0, 2, 1, 3)
    return shaped.reshape(rows // BS * (cols // BS), BS * BS)


def rank_within(dest):
    entries = dest.shape[-1]
    order = jnp.arange(entries, dtype=jnp.int32)
    same = (dest[..., :, None] == dest[..., None, :]) & (order[None, :] < order[:, None])
    return jnp.sum(same.astype(jnp.int32), axis=-1)


def shards(
    sign_iterate,
    sign_square,
    pattern_x,
    pattern_y,
    pattern_product,
    orbital_energy,
    pair_dest,
    pair_block,
    force_h,
    force_s,
):
    rows_x, cols_x = sign_iterate.shape
    xmask = masked_tile(sign_iterate, pattern_x)
    ymask = masked_tile(sign_square, pattern_y)
    y_whole = lax.all_gather(ymask, "row", axis=0, tiled=True)
    product = jnp.dot(
        lax.all_gather(xmask, "col", axis=1, tiled=True),
        y_whole,
        preferred_element_type=jnp.float32,
    )
    product = masked_tile(product, pattern_product)
    xnew = 1.5 * xmask.astype(jnp.float32) - 0.5 * product
    sign_next = xnew.astype(jnp.bfloat16)
    global_rows = lax.axis_index("row") * rows_x + jnp.arange(rows_x, dtype=jnp.int32)
    global_cols = lax.axis_index("col") * cols_x + jnp.arange(cols_x, dtype=jnp.int32)
    identity = (global_rows[:, None] == global_cols[None, :]).astype(jnp.float32)
    density = (0.5 * identity - 0.5 * xnew).astype(jnp.bfloat16)
    dens_blocks = tile_blocks(density)
    n_rows = lax.axis_size("row")
    n_cols = lax.axis_size("col")
    devices = n_rows * n_cols
    slots = devices * CAP
    local_rows = rows_x // BS
    dest = pair_dest[0, :, 0]
    wanted = pair_block[0]
    rank = rank_within(dest)
    slot = dest * CAP + rank
    pick_slot = (jnp.arange(slots, dtype=jnp.int32)[:, None] == slot[None, :]).astype(jnp.bfloat16)
    pick_block = (
        wanted[:, None] == jnp.arange(dens_blocks.shape[0], dtype=jnp.int32)[None, :]
    ).astype(jnp.bfloat16)
    routing_table = jnp.dot(pick_slot, pick_block, preferred_element_type=jnp.float32).astype(
        jnp.bfloat16
    )
    send_dens = jnp.dot(routing_table, dens_blocks, preferred_element_type=jnp.float32).astype(
        jnp.bfloat16
    )
    pick_row = ((wanted // QB)[:, None] == jnp.arange(local_rows, dtype=jnp.int32)[None, :]).astype(
        jnp.bfloat16
    )
    slot_rows = jnp.dot(pick_slot, pick_row, preferred_element_type=jnp.float32).astype(
        jnp.bfloat16
    )
    send_energy = jnp.dot(
        slot_rows, orbital_energy.reshape(local_rows, BS), preferred_element_type=jnp.float32
    ).astype(jnp.bfloat16)
    payload = jnp.concatenate([send_dens.reshape(slots, BS, BS), send_energy[:, None, :]], axis=1)
    height = BS + 1
    received = lax.all_to_all(
        payload.reshape(devices, CAP, height * BS),
        ("row", "col"),
        split_axis=0,
        concat_axis=0,
        tiled=True,
    )
    received = received.reshape(slots, height, BS)
    recv_dens = received[:, :BS, :]
    energies = received[:, BS, :].astype(jnp.float32)
    h_term = jnp.einsum("sab,sab->s", recv_dens, force_h, preferred_element_type=jnp.float32)
    s_rows = jnp.einsum("sab,sab->sa", recv_dens, force_s, preferred_element_type=jnp.float32)
    forces = h_term - jnp.sum(energies * s_rows, axis=1)
    return (sign_next, forces)


ROWS = 4
COLS = 8
DEVICES = ROWS * COLS
LINE = 4
CHUNKS = 4
TALL = 8
STEP = 256
PIECES = 2
KEPT = 16
HALF = 512


def kernel(
    room,
    pat_x,
    pat_y,
    pat_p,
    dest,
    wanted,
    pat_tile,
    energy,
    x_hbm,
    y_hbm,
    h_hbm,
    s_hbm,
    sign_hbm,
    parts,
    short,
    xraw,
    lines,
    spill_out,
    spill_in,
    xg,
    yg,
    acc,
    dens,
    sgn,
    hbuf,
    sbuf,
    wbuf,
    outbox,
    inbox,
    e_out,
    e_in,
    e_table,
    e_rows,
    t_out,
    t_in,
    pats,
    ahead,
    listed,
    place,
    tallies,
    table,
    local_sem,
    up_sem,
    down_sem,
    twin_sem,
    x_sem,
    tx_sem,
    ysend_sem,
    y_sem,
    e_sem,
    esend_sem,
    d_sem,
    dsend_sem,
    t_sem,
    tsend_sem,
    spill_sem,
    rows_sem,
    rsend_sem,
):
    blocks = QB * TALL
    piece = room // PIECES
    spill = blocks - room
    r = lax.axis_index("row")
    c = lax.axis_index("col")
    me = r * COLS + c
    z = c // 2
    core = c % 2
    row_x = r + 1 - 2 * (r % 2)
    row_y = (r + 2) % 4

    barrier = pltpu.get_barrier_semaphore()

    def greet(i, carry):
        other = (me + i) % DEVICES
        pl.semaphore_signal(
            barrier, inc=1, device_id=(other // COLS, other % COLS), device_id_type=MESH
        )
        return carry

    lax.fori_loop(1, DEVICES, greet, 0)

    for j in range(QB):
        pltpu.make_async_copy(
            x_hbm.at[:, :, j * BS : (j + 1) * BS],
            xraw.at[pl.ds(j * TALL, TALL)],
            local_sem.at[0],
        ).start()
    whole = xraw.at[pl.ds(0, blocks)]
    get_x = pltpu.make_async_copy(whole, whole, local_sem.at[0])
    get_y = pltpu.make_async_copy(y_hbm, yg.at[r], local_sem.at[1])
    get_h = pltpu.make_async_copy(h_hbm, hbuf, local_sem.at[2])
    get_s = pltpu.make_async_copy(s_hbm, sbuf, local_sem.at[3])
    get_y.start()
    get_h.start()
    get_s.start()

    def loop(lo, hi, body):
        def step(i, carry):
            body(i)
            return carry

        lax.fori_loop(lo, hi, step, 0)

    half = blocks + 1

    def x_copy(src, dst, ch, col, send_sem, recv_sem):
        rows = pl.ds(core * half + ch * piece, piece)
        return pltpu.make_async_remote_copy(
            src_ref=lines[src].at[rows],
            dst_ref=lines[dst].at[rows],
            send_sem=send_sem,
            recv_sem=recv_sem,
            device_id=(r, col),
            device_id_type=MESH,
        )

    def up(d, ch):
        return x_copy(d, d + 1, ch, c + 2, up_sem.at[d, ch], x_sem.at[d + 1, ch])

    def down(d, ch):
        to = d + LINE
        src = to - 1 if d else 0
        return x_copy(src, to, ch, c - 2, down_sem.at[d, ch], x_sem.at[to, ch])

    twin_col = c + 1 - 2 * core

    def twin(i, ch):
        return x_copy(i, i, ch, twin_col, twin_sem.at[i, ch], tx_sem.at[i, ch])

    def from_twin(i, ch):
        rows = pl.ds((1 - core) * half + ch * piece, piece)
        return pltpu.make_async_copy(lines[i].at[rows], lines[i].at[rows], tx_sem.at[i, ch])

    def y_copy(owner, half, to, number):
        block = yg.at[owner, pl.ds(half * HALF, HALF)]
        return pltpu.make_async_remote_copy(
            src_ref=block,
            dst_ref=block,
            send_sem=ysend_sem.at[number],
            recv_sem=y_sem.at[owner, half],
            device_id=(to, c),
            device_id_type=MESH,
        )

    t_out[...] = jnp.zeros_like(t_out)
    t_out[0:QB, 0:TALL] = pat_tile[...]
    number = jnp.int32(0)
    for b in range(blocks):
        number = number + pat_x[b // TALL, b % TALL]
        ahead[b] = number
    count = number

    def seek(t):
        found = jnp.int32(0)
        for b in range(blocks):
            found = found + (ahead[b] <= t).astype(jnp.int32)
        listed[t] = found

    loop(0, blocks, seek)
    xraw[blocks] = jnp.zeros((BS, BS), jnp.bfloat16)

    def at_least(n, low):
        return low + (n > low).astype(jnp.int32) * (n - low)

    get_x.wait()

    early = KEPT if spill else room

    def compact(t):
        lines[0][core * half + t] = xraw[listed[t]]

    loop(0, early, compact)
    for t in range(spill):
        spill_out[t] = xraw[listed[room + t]]
    if spill:
        spill_in[spill] = jnp.zeros((BS, BS), jnp.bfloat16)
    pl.semaphore_wait(barrier, DEVICES - 1)

    def t_copy(col):
        return pltpu.make_async_remote_copy(
            src_ref=t_out,
            dst_ref=t_in.at[c],
            send_sem=tsend_sem,
            recv_sem=t_sem,
            device_id=(r, col),
            device_id_type=MESH,
        )

    loop(1, COLS, lambda i: t_copy((c + i) % COLS).start())
    pltpu.make_async_copy(t_out, t_in.at[c], t_sem).start()

    def send_x(ch):
        @pl.when(z < LINE - 1)
        def _():
            up(0, ch).start()

        @pl.when(z > 0)
        def _():
            down(0, ch).start()

        twin(0, ch).start()

    hand_over = None
    if spill:
        hand_over = pltpu.make_async_remote_copy(
            src_ref=spill_out,
            dst_ref=spill_in.at[pl.ds(0, spill)],
            send_sem=spill_sem.at[0],
            recv_sem=spill_sem.at[1],
            device_id=(r, twin_col),
            device_id_type=MESH,
        )
        hand_over.start()
    send_x(0)
    get_y.wait()

    def mask_y(i):
        rows = pl.ds(i * BS, BS)
        for j in range(QB):
            cols = slice(j * BS, (j + 1) * BS)
            keep = pat_y[j, i].astype(jnp.float32)
            yg[r, rows, cols] = (yg[r, rows, cols].astype(jnp.float32) * keep).astype(jnp.bfloat16)

    loop(0, TALL, mask_y)
    y_copy(r, 0, row_x, 0).start()
    y_copy(r, 1, row_y, 1).start()
    y_copy(r, 1, row_x, 2).start()
    y_copy(r, 0, row_y, 3).start()

    if spill:
        hand_over.wait_recv()
        used = at_least(count, KEPT)

        def fill(t):
            own = (t < count).astype(jnp.int32)
            extra = spill_in[own * spill + (1 - own) * (t - used) * (t >= used).astype(jnp.int32)]
            lines[0][core * half + t] = xraw[listed[t]] + extra

        loop(early, room, fill)
    loop(1, PIECES, send_x)
    def mask_x(i):
        rows = pl.ds(i * BS, BS)
        for j in range(QB):
            keep = pat_x[j, i].astype(jnp.float32)
            block = xraw[j * TALL + i].astype(jnp.float32) * keep
            xg[c, rows, j * BS : (j + 1) * BS] = block.astype(jnp.bfloat16)

    loop(0, TALL, mask_x)

    def find(o):
        seen = jnp.int32(0)
        slots = [jnp.int32(blocks)] * CAP
        for p in range(dest.shape[1]):
            hit = (dest[0, p] == o).astype(jnp.int32)
            for k in range(CAP):
                first_seen = hit * (seen == k).astype(jnp.int32)
                slots[k] = slots[k] + first_seen * (wanted[0, p] - blocks)
            seen = seen + hit
        for k in range(CAP):
            table[o * CAP + k] = slots[k]

    loop(0, DEVICES, find)
    lanes = lax.broadcasted_iota(jnp.int32, (1, BS), 1)

    def pack(o):
        line = jnp.full((1, BS), count)
        for k in range(CAP):
            line = jnp.where(lanes == k, table[o * CAP + k], line)
        e_out[o] = line

    loop(0, DEVICES, pack)

    def e_copy(o):
        return pltpu.make_async_remote_copy(
            src_ref=e_out.at[o],
            dst_ref=e_in.at[me],
            send_sem=esend_sem,
            recv_sem=e_sem,
            device_id=(o // COLS, o % COLS),
            device_id_type=MESH,
        )

    loop(1, DEVICES, lambda i: e_copy((me + i) % DEVICES).start())
    pltpu.make_async_copy(e_out.at[me], e_in.at[me], e_sem).start()

    for i in range(ROWS):
        e_rows[i, TALL : 2 * TALL, :] = jnp.zeros((TALL, BS), jnp.float32)
    own_rows = e_rows.at[r, pl.ds(0, TALL)]
    own_rows[...] = energy[...].astype(jnp.float32)

    def row_copy(i):
        return pltpu.make_async_remote_copy(
            src_ref=own_rows,
            dst_ref=own_rows,
            send_sem=rsend_sem.at[i],
            recv_sem=rows_sem.at[r],
            device_id=((r + i) % ROWS, c),
            device_id_type=MESH,
        )

    def row_arrival(i):
        other = (r + i) % ROWS
        ref = e_rows.at[other, pl.ds(0, TALL)]
        return pltpu.make_async_copy(ref, ref, rows_sem.at[other])

    for i in range(1, ROWS):
        row_copy(i).start()

    def pass_on(d, ch):
        @pl.when(z >= d)
        def _():
            up(d - 1, ch).wait_recv()
            if d < LINE - 1:

                @pl.when(z < LINE - 1)
                def _():
                    up(d, ch).start()

            twin(d, ch).start()

        @pl.when(z + d < LINE)
        def _():
            down(d - 1, ch).wait_recv()
            if d < LINE - 1:

                @pl.when(z > 0)
                def _():
                    down(d, ch).start()

            twin(LINE - 1 + d, ch).start()

    def wait_twin(i):
        loop(0, PIECES, lambda ch: from_twin(i, ch).wait())

    def expand(ref, panel, ch):
        for i in range(STEP // BS):
            row = ch * (STEP // BS) + i
            for j in range(QB):
                block = ref[place[panel, j * TALL + row]]
                xg[panel, pl.ds(row * BS, BS), j * BS : (j + 1) * BS] = block

    def multiply(zp, ch):
        rows = pl.ds(ch * STEP, STEP)
        return jnp.dot(
            xg[2 * zp, rows, :], yg[zp, 0:HALF, :], preferred_element_type=jnp.float32
        ) + jnp.dot(
            xg[2 * zp + 1, rows, :], yg[zp, HALF : 2 * HALF, :], preferred_element_type=jnp.float32
        )

    def add(d):
        def panels(zp, i):
            wait_twin(i)

            def one(ch):
                expand(lines[i], 2 * zp, ch)
                expand(lines[i], 2 * zp + 1, ch)
                acc[pl.ds(ch * STEP, STEP), :] += multiply(zp, ch)

            loop(0, CHUNKS, one)

        @pl.when(z >= d)
        def _():
            panels(z - d, d)

        @pl.when(z + d < LINE)
        def _():
            panels(z + d, LINE - 1 + d)

    loop(0, 1, lambda ch: pass_on(1, ch))

    pltpu.make_async_copy(t_in, t_in, t_sem).wait()
    get_pats = pltpu.make_async_copy(t_in, pats, local_sem.at[5])
    get_pats.start()
    get_pats.wait()

    for ref in lines:
        ref[blocks] = jnp.zeros((BS, BS), jnp.bfloat16)
        ref[half + blocks] = jnp.zeros((BS, BS), jnp.bfloat16)

    def tally(panel):
        number = jnp.int32(0)
        for b in range(blocks):
            number = number + pats[panel, b // TALL, b % TALL]
        tallies[panel] = number

    loop(0, COLS, tally)

    def locate(panel):
        kind = panel % 2
        start = kind * half
        beyond = (1 - kind) * half + at_least(tallies[panel + 1 - 2 * kind], KEPT)
        last_spot = (1 - kind) * half + blocks
        number = jnp.int32(0)
        for b in range(blocks):
            on = pats[panel, b // TALL, b % TALL]
            fits = (number < room).astype(jnp.int32)
            past = beyond + number - room
            past = past - (past > last_spot).astype(jnp.int32) * (past - last_spot)
            spot = fits * (start + number) + (1 - fits) * past
            place[panel, b] = on * spot + (1 - on) * blocks
            number = number + on

    loop(0, COLS, locate)

    loop(1, PIECES, lambda ch: pass_on(1, ch))

    dens[QB * 8] = jnp.zeros((BS, BS), jnp.bfloat16)
    get_h.wait()
    get_s.wait()
    pltpu.make_async_copy(e_in, e_in, e_sem).wait()
    get_table = pltpu.make_async_copy(e_in, e_table, local_sem.at[5])
    get_table.start()
    get_table.wait()
    for i in range(1, ROWS):
        row_arrival(i).wait()

    eye = lax.broadcasted_iota(jnp.int32, (BS, BS), 0) == lax.broadcasted_iota(
        jnp.int32, (BS, BS), 1
    )

    def weigh(src, carry):
        for k in range(CAP):
            line = e_rows[src // COLS, pl.ds(e_table[src, 0, k] // QB, 1), :]
            line = jnp.broadcast_to(line, (BS, BS))
            col = jnp.sum(jnp.where(eye, line, 0.0), axis=1, keepdims=True)
            s = src * CAP + k
            wbuf[s] = hbuf[s].astype(jnp.float32) - col * sbuf[s].astype(jnp.float32)
        return carry

    lax.fori_loop(0, DEVICES, weigh, 0)

    wrong = jnp.int32(0)
    for src in range(DEVICES):
        mine, other = e_table[src, 0, CAP], e_table[src + 1 - 2 * (src % 2), 0, CAP]
        over = (mine > room).astype(jnp.int32) * (mine - room)
        free = (other < room).astype(jnp.int32) * (room - at_least(other, KEPT))
        wrong = wrong + (over > free).astype(jnp.int32)
    short[0] = (wrong > 0).astype(jnp.int32)

    y_copy(row_x, 0, r, 0).wait_recv()
    y_copy(row_x, 0, row_y, 4).start()
    y_copy(row_y, 1, r, 1).wait_recv()
    y_copy(row_y, 1, row_x, 5).start()
    loop(0, PIECES, lambda ch: pass_on(2, ch))
    y_copy(row_x, 1, r, 2).wait_recv()
    y_copy(row_y, 0, r, 3).wait_recv()
    row_d = 3 - r
    y_copy(row_d, 0, r, 4).wait_recv()
    y_copy(row_d, 1, r, 5).wait_recv()
    wait_twin(0)

    def first(ch):
        expand(lines[0], 2 * z + 1 - core, ch)
        acc[pl.ds(ch * STEP, STEP), :] = multiply(z, ch)

    loop(0, CHUNKS, first)
    add(1)
    add(2)

    eye_f = eye.astype(jnp.float32)

    def finish(ch):
        for i in range(STEP // BS):
            block_row = ch * (STEP // BS) + i
            rows = pl.ds(ch * STEP + i * BS, BS)
            for j in range(QB):
                cols = slice(j * BS, (j + 1) * BS)
                keep = pat_p[j, block_row].astype(jnp.float32)
                xnew = 1.5 * xg[c, rows, cols].astype(jnp.float32) - 0.5 * (acc[rows, cols] * keep)
                sgn[rows, cols] = xnew.astype(jnp.bfloat16)
                on = jnp.where(r * 8 + block_row == c * QB + j, 0.5, 0.0).astype(jnp.float32)
                dens[block_row * QB + j] = (on * eye_f - 0.5 * xnew).astype(jnp.bfloat16)

    loop(0, PIECES, lambda ch: pass_on(3, ch))
    add(3)
    loop(0, CHUNKS, finish)

    put = pltpu.make_async_copy(sgn, sign_hbm, local_sem.at[4])
    put.start()

    def d_copy(o, src):
        return pltpu.make_async_remote_copy(
            src_ref=outbox.at[o],
            dst_ref=inbox.at[src],
            send_sem=dsend_sem,
            recv_sem=d_sem.at[src],
            device_id=(o // COLS, o % COLS),
            device_id_type=MESH,
        )

    def sent(ch):
        twin(0, ch).wait_send()
        for d in range(LINE):

            @pl.when(z >= d)
            def _(d=d):
                if d:
                    twin(d, ch).wait_send()
                if d < LINE - 1:

                    @pl.when(z < LINE - 1)
                    def _():
                        up(d, ch).wait_send()

            @pl.when(z + d < LINE)
            def _(d=d):
                if d:
                    twin(LINE - 1 + d, ch).wait_send()
                if d < LINE - 1:

                    @pl.when(z > 0)
                    def _():
                        down(d, ch).wait_send()

    inner = z * (LINE - 1 - z) // 2
    near = z + 1 - 2 * (z % 2)
    far = (z + 2) % LINE
    planes = (
        LINE - 1 - z,
        far + inner * (z - far),
        near + inner * (far - near),
        z + inner * (near - z),
    )
    for n, zz in enumerate(planes):
        if n == 2:
            loop(0, PIECES, sent)

        def send(j, zz=zz):
            o = (r + j // 2) % ROWS * COLS + zz * 2 + (core + j) % 2

            @pl.when(o != me)
            def _():
                for k in range(CAP):
                    outbox[o, k] = dens[table[o * CAP + k]]
                d_copy(o, me).start()

        loop(0, COLS, send)

    def force(s, block):
        parts[pl.ds(s, 1), :] = jnp.sum(block.astype(jnp.float32) * wbuf[s], axis=0, keepdims=True)

    for k in range(CAP):
        force(me * CAP + k, dens[table[me * CAP + k]])

    for zz in (1, 2, 0, 3):

        def take(j, zz=zz):
            src = (r + ROWS - j // 2) % ROWS * COLS + zz * 2 + (core + j) % 2

            @pl.when(src != me)
            def _():
                d_copy(src, src).wait_recv()
                for k in range(CAP):
                    force(src * CAP + k, inbox[src, k])

        loop(0, COLS, take)

    if spill:
        hand_over.wait_send()
    for i in range(1, ROWS):
        row_copy(i).wait_send()
    y_copy(r, 0, row_x, 0).wait_send()
    y_copy(r, 1, row_y, 1).wait_send()
    y_copy(r, 1, row_x, 2).wait_send()
    y_copy(r, 0, row_y, 3).wait_send()
    y_copy(row_x, 0, row_y, 4).wait_send()
    y_copy(row_y, 1, row_x, 5).wait_send()
    out = t_in.at[pl.ds(0, COLS - 1)]
    pltpu.make_async_copy(out, out, tsend_sem).wait()
    out = e_out.at[pl.ds(0, DEVICES - 1)]
    pltpu.make_async_copy(out, out, esend_sem).wait()
    out = outbox.at[pl.ds(0, DEVICES - 1)]
    pltpu.make_async_copy(out, out, dsend_sem).wait()
    put.wait()


def fused(
    room,
    number,
    sign_iterate,
    sign_square,
    pattern_x,
    pattern_y,
    pattern_product,
    orbital_energy,
    pair_dest,
    pair_block,
    force_h,
    force_s,
):
    slots = DEVICES * CAP
    blocks = QB * TALL
    vmem = pl.BlockSpec(memory_space=pltpu.VMEM)
    smem = pl.BlockSpec(memory_space=pltpu.SMEM)
    hbm = pl.BlockSpec(memory_space=pl.ANY)
    bf16, f32, i32 = jnp.bfloat16, jnp.float32, jnp.int32
    dma = pltpu.SemaphoreType.DMA
    tile = sign_iterate.shape
    return pl.pallas_call(
        functools.partial(kernel, room),
        out_shape=(
            jax.ShapeDtypeStruct(tile, bf16),
            jax.ShapeDtypeStruct((slots, BS), f32),
            jax.ShapeDtypeStruct((1,), i32),
        ),
        in_specs=[smem] * 5 + [vmem] * 2 + [hbm] * 4,
        out_specs=(hbm, vmem, smem),
        scratch_shapes=[
            pltpu.VMEM((blocks + 1, BS, BS), bf16),
            [pltpu.VMEM((2 * blocks + 2, BS, BS), bf16)] * (2 * LINE - 1),
            pltpu.VMEM((max(blocks - room, 1), BS, BS), bf16),
            pltpu.VMEM((blocks - room + 1, BS, BS), bf16),
            pltpu.VMEM((COLS, *tile), bf16),
            pltpu.VMEM((ROWS, *tile), bf16),
            pltpu.VMEM(tile, f32),
            pltpu.VMEM((blocks + 1, BS, BS), bf16),
            pltpu.VMEM(tile, bf16),
            pltpu.VMEM((slots, BS, BS), bf16),
            pltpu.VMEM((slots, BS, BS), bf16),
            pltpu.VMEM((slots, BS, BS), f32),
            pltpu.VMEM((DEVICES, CAP, BS, BS), bf16),
            pltpu.VMEM((DEVICES, CAP, BS, BS), bf16),
            pltpu.VMEM((DEVICES, 1, BS), i32),
            pltpu.VMEM((DEVICES, 1, BS), i32),
            pltpu.SMEM((DEVICES, 1, BS), i32),
            pltpu.VMEM((ROWS, 2 * TALL, BS), f32),
            pltpu.VMEM((QB, BS), i32),
            pltpu.VMEM((COLS, QB, BS), i32),
            pltpu.SMEM((COLS, QB, BS), i32),
            pltpu.SMEM((blocks,), i32),
            pltpu.SMEM((blocks,), i32),
            pltpu.SMEM((COLS, blocks), i32),
            pltpu.SMEM((COLS,), i32),
            pltpu.SMEM((slots,), i32),
            dma((6,)),
            dma((LINE - 1, PIECES)),
            dma((LINE - 1, PIECES)),
            dma((2 * LINE - 1, PIECES)),
            dma((2 * LINE - 1, PIECES)),
            dma((2 * LINE - 1, PIECES)),
            dma((6,)),
            dma((ROWS, 2)),
            dma,
            dma,
            dma((DEVICES,)),
            dma,
            dma,
            dma,
            dma((2,)),
            dma((ROWS,)),
            dma((ROWS,)),
        ],
        compiler_params=pltpu.CompilerParams(
            collective_id=number, has_side_effects=True, vmem_limit_bytes=60 * 1024 * 1024
        ),
        cost_estimate=pl.CostEstimate(
            flops=2 * 1024 * 4096 * 512, bytes_accessed=8 * 1024 * 1024, transcendentals=0
        ),
        name=f"room_{room}",
    )(
        pattern_x.T,
        pattern_y.T,
        pattern_product.T,
        pair_dest[:, :, 0],
        pair_block,
        pattern_x.T,
        orbital_energy.reshape(-1, BS),
        sign_iterate.reshape(TALL, BS, tile[1]),
        sign_square,
        force_h,
        force_s,
    )


ROOM = 22


def adaptive(*arrays):
    sign_next, parts, short = fused(ROOM, 0, *arrays)
    sign_next, parts = lax.switch(
        short[0],
        (lambda: (sign_next, parts), lambda: tuple(fused(QB * TALL, 1, *arrays)[:2])),
    )
    return sign_next, jnp.sum(parts, axis=1)


def solution(mesh):
    in_specs = (
        P("row", "col"),
        P("row", "col"),
        P("row", "col"),
        P("row", "col"),
        P("row", "col"),
        P("row"),
        P(("row", "col"), None, None),
        P(("row", "col"), None),
        P(("row", "col"), None, None),
        P(("row", "col"), None, None),
    )
    out_specs = (P("row", "col"), P(("row", "col")))
    body = adaptive if (mesh.shape["row"], mesh.shape["col"]) == (ROWS, COLS) else shards
    return jax.shard_map(body, mesh=mesh, in_specs=in_specs, out_specs=out_specs, check_vma=False)
```
